256 devices in a mesh: gx: 32 (over x, y, core), gy: 8 (over z).
Axes of the slice: x: 4, y: 4, z: 8, core: 2. Of those that a mesh axis runs over, the one named last changes fastest.
Arguments:
- fine_field: bfloat16 [64, 128, 64, 128], P('gx', 'gy'), may hold values from -6 to 6
- down_weight: bfloat16 [8, 128, 256], replicated, may hold values from -0.1875 to 0.1875
- conv_weight: bfloat16 [27, 256, 256], replicated, may hold values from -0.078125 to 0.078125
- coarse_cotangent: bfloat16 [32, 64, 32, 256], P('gx', 'gy'), may hold values from -6 to 6
Outputs:
- fine_grad: bfloat16 [64, 128, 64, 128], P('gx', 'gy')
- conv_weight_grad: bfloat16 [27, 256, 256], replicated
- down_weight_grad: bfloat16 [8, 128, 256], replicated
The draws below stay inside these ranges and needn't reach their ends.
All inputs are finite; a program needn't handle non-finite values.
Results may differ from the reference program's by a relative error of at most 0.0065.
Values may be sent and summed in bfloat16 or wider, within the bound.
A program may use at most 64 MiB of HBM per device.

```python
import jax
import jax.numpy as jnp

C1 = 128
C2 = 256
NX = 32
NY = 64
NZ = 32


def block_scale(stream_key, shape, split, low, top_value):
    level = 1.0
    for axis_at, shards_of in split:
        heights = jax.random.uniform(jax.random.fold_in(jax.random.fold_in(stream_key, 6), axis_at), (shards_of,), jnp.float32, low / len(split), top_value / len(split))
        level = level * jnp.repeat(jnp.exp(heights), shape[axis_at] // shards_of).reshape((-1,) + (1,) * (len(shape) - 1 - axis_at))
    return level


def scatter_about(stream_key, extent, deviation, limit, shards=(), dtype=jnp.bfloat16):
    array = jax.random.normal(stream_key, extent, jnp.float32) * deviation
    if len(shards) > 0:
        array = block_scale(stream_key, extent, shards, -0.22, 0.18) * array
    return jnp.clip(array, min=-limit, max=limit).astype(dtype)


def setup_inputs(seed: int = 0) -> dict:
    keys = jax.random.split(jax.random.key(seed), 5)
    return {
        "fine_field": scatter_about(keys[0], (2 * NX, 2 * NY, 2 * NZ, C1), 1.0, 6.0, ((0, 32), (1, 8))),
        "down_weight": scatter_about(keys[1], (8, C1, C2), (8 * C1) ** -0.5, 0.1875),
        "conv_weight": scatter_about(keys[2], (27, C2, C2), (27 * C2) ** -0.5, 0.078125),
        "coarse_cotangent": scatter_about(keys[3], (NX, NY, NZ, C2), 1.0, 6.0, ((0, 32), (1, 8))),
    }


def to_blocks(field, count_x, count_y, count_z, width):
    shaped = field.reshape(count_x, 2, count_y, 2, count_z, 2, width)
    return shaped.transpose(0, 2, 4, 1, 3, 5, 6).reshape(count_x * count_y * count_z, 8 * width)


def from_blocks(blocks, count_x, count_y, count_z, width):
    shaped = blocks.reshape(count_x, count_y, count_z, 2, 2, 2, width)
    return shaped.transpose(0, 3, 1, 4, 2, 5, 6).reshape(2 * count_x, 2 * count_y, 2 * count_z, width)


def reference(fine_field, down_weight, conv_weight, coarse_cotangent):
    blocks = to_blocks(fine_field, NX, NY, NZ, C1)
    down_flat = down_weight.reshape(8 * C1, C2)
    hidden = jnp.dot(blocks, down_flat, preferred_element_type=jnp.float32).astype(jnp.bfloat16)
    padded = jnp.pad(hidden.reshape(NX, NY, NZ, C2), ((1, 1), (1, 1), (1, 1), (0, 0)))
    preact = jnp.zeros((NX * NY * NZ, C2), jnp.float32)
    for first in range(3):
        for second in range(3):
            for third in range(3):
                piece = padded[first:first + NX, second:second + NY, third:third + NZ].reshape(-1, C2)
                preact = preact + jnp.dot(piece, conv_weight[9 * first + 3 * second + third], preferred_element_type=jnp.float32)
    sig = jax.nn.sigmoid(preact)
    cotangent = coarse_cotangent.reshape(-1, C2).astype(jnp.float32)
    pre_grad = (cotangent * (sig * (1.0 + preact * (1.0 - sig)))).astype(jnp.bfloat16)
    grad_padded = jnp.pad(pre_grad.reshape(NX, NY, NZ, C2), ((1, 1), (1, 1), (1, 1), (0, 0)))
    conv_terms = []
    back = jnp.zeros((NX * NY * NZ, C2), jnp.float32)
    for first in range(3):
        for second in range(3):
            for third in range(3):
                piece = padded[first:first + NX, second:second + NY, third:third + NZ].reshape(-1, C2)
                conv_terms.append(jnp.dot(piece.T, pre_grad, preferred_element_type=jnp.float32))
                moved = grad_padded[2 - first:2 - first + NX, 2 - second:2 - second + NY, 2 - third:2 - third + NZ].reshape(-1, C2)
                back = back + jnp.dot(moved, conv_weight[9 * first + 3 * second + third].T, preferred_element_type=jnp.float32)
    conv_weight_grad = jnp.stack(conv_terms).astype(jnp.bfloat16)
    hidden_grad = (cotangent + back).astype(jnp.bfloat16)
    fine_flat = jnp.dot(hidden_grad, down_flat.T, preferred_element_type=jnp.float32).astype(jnp.bfloat16)
    fine_grad = from_blocks(fine_flat, NX, NY, NZ, C1)
    down_weight_grad = jnp.dot(blocks.T, hidden_grad, preferred_element_type=jnp.float32).reshape(8, C1, C2).astype(jnp.bfloat16)
    return fine_grad, conv_weight_grad, down_weight_grad
```

```python
import jax
import jax.numpy as jnp
from jax import lax
from jax.experimental import pallas as pl
from jax.experimental.pallas import tpu as pltpu
from jax.sharding import PartitionSpec as P

MESH = pl.DeviceIdType.MESH
BF = jnp.bfloat16
F32 = jnp.float32

STREAMS = ((0, 7, True), (7, 7, False), (14, 7, True), (21, 6, False), (27, 4, True))
CONV_STREAMS = 4


def dot(a, b):
    return jnp.dot(a, b, preferred_element_type=F32)


def dot_t(a, b):
    return lax.dot_general(a, b, (((1,), (1,)), ((), ())), preferred_element_type=F32)


def iotas(n):
    return lax.broadcasted_iota(jnp.int32, (n, n), 0), lax.broadcasted_iota(jnp.int32, (n, n), 1)


def ones_where(mask):
    return jnp.where(mask, 1.0, 0.0).astype(BF)


def kernel(
    fine, down_w, conv_w, cot, fine_out, conv_out, down_out,
    x_mat, x_t, q, hs, ht, gp, gs, sums, part, part_in, r1, y1, r2, z1, r3, out,
    halo_s, halo_r, step_s, step_r, out_sem,
):
    gx, z = lax.axis_index("gx"), lax.axis_index("gy")
    px, py, c = gx // 8, (gx // 2) % 4, gx % 2

    def at(dx, dz):
        return ((gx + dx + 32) % 32, (z + dz + 8) % 8)

    def on_x(k):
        return ((((px + k) % 4) * 4 + py) * 2 + c, z)

    def on_y(k):
        return ((px * 4 + (py + k) % 4) * 2 + c, z)

    def on_z(k):
        return (gx, (z + k) % 8)

    partner = (gx + 1 - 2 * c, z)
    far = 4 * c - 2

    greeted = [at(dx, dz) for dx in (-1, 0, 1) for dz in (-1, 0, 1) if (dx, dz) != (0, 0)]
    greeted += [at(far * w, dz) for w in (1, -1) for dz in (-1, 0, 1)]
    greeted += [on_x(k) for k in (1, 2, 3)] + [on_y(k) for k in (1, 2, 3)]
    greeted += [on_z(k) for k in range(2, 7)]
    barrier = pltpu.get_barrier_semaphore()
    for device in greeted:
        pl.semaphore_signal(barrier, inc=1, device_id=device, device_id_type=MESH)

    started = []

    def send(src, dst, s_sem, r_sem, device):
        copy = pltpu.make_async_remote_copy(
            src_ref=src, dst_ref=dst, send_sem=s_sem, recv_sem=r_sem, device_id=device, device_id_type=MESH
        )
        copy.start()
        started.append(copy)
        return copy

    row, col = iotas(256)

    def target(r):
        group, j, k = r // 64, (r // 32) % 2, r % 32
        return (j * 2 + group // 2) * 64 + 2 * k + group % 2

    sort = ones_where(col == target(row))
    for a in range(2):
        for block in range(4):
            rows = fine[a, 4 * block : 4 * block + 4].reshape(256, 128)
            sorted_rows = dot(sort, rows).astype(BF)
            for group in range(4):
                lane = (4 * a + group) * 128
                x_mat[64 * block : 64 * block + 64, lane : lane + 128] = sorted_rows[64 * group : 64 * group + 64]
    hidden = dot(x_mat[...], down_w[...].reshape(1024, 256)).astype(BF)
    mine = 1 + c
    for half in range(2):
        q[mine, half, 32:288, :] = hidden[:, 128 * half : 128 * half + 128]

    pl.semaphore_wait(barrier, len(greeted))

    whole, low, high = pl.ds(32, 256), pl.ds(256, 32), pl.ds(32, 32)
    first, last = pl.ds(0, 32), pl.ds(288, 32)
    hidden_copies = []
    n = 0
    for dx, plane in ((1, 1 - c), (-1, 3 - c), (0, mine)):
        for dz, src, dst in ((0, whole, whole), (1, low, first), (-1, high, last)):
            if (dx, dz) != (0, 0):
                hidden_copies.append(
                    send(q.at[mine, :, src], q.at[plane, :, dst], halo_s.at[n], halo_r.at[n], at(dx, dz))
                )
                n += 1
    far_copies = []
    for dz, src, dst in ((0, whole, whole), (1, low, first), (-1, high, last)):
        far_copies.append(
            send(q.at[mine, c, src], q.at[3 - 3 * c, c, dst], halo_s.at[n], halo_r.at[n], at(far, dz))
        )
        n += 1

    r128, c128 = iotas(128)
    eye = ones_where(r128 == c128)
    for t in range(8):
        x_t[t] = dot_t(eye, x_mat[:, 128 * t : 128 * t + 128]).astype(BF)

    before = ones_where((col == row - 1) & (row % 32 != 0))
    after = ones_where((col == row + 1) & (row % 32 != 31))

    for copy in hidden_copies:
        copy.wait_recv()
    top, bottom, left, right = z > 0, z < 7, gx > 0, gx < 31
    for a, valid in ((0, left), (1, None), (2, right)):
        if valid is not None:
            q[c + a, :, 32:288] = jnp.where(valid, q[c + a, :, 32:288], jnp.zeros((2, 256, 128), BF))
        for rows, ok in ((slice(0, 32), top), (slice(288, 320), bottom)):
            both = ok if valid is None else jnp.logical_and(ok, valid)
            q[c + a, :, rows] = jnp.where(both, q[c + a, :, rows], jnp.zeros((2, 32, 128), BF))
    acc = None
    for a in range(3):
        plane = jnp.concatenate([q[c + a, 0], q[c + a, 1]], axis=1)
        for i, shift in ((0, before), (1, after)):
            hs[i, a, 0:256] = dot(shift, plane[0:256]).astype(BF)
            hs[i, a, 256:320] = dot(shift[0:64, 0:64], plane[256:320]).astype(BF)
        pieces = []
        for b in range(3):
            rows = slice(32 * b, 32 * b + 256)
            pieces += [hs[0, a, rows], plane[rows], hs[1, a, rows]]
        term = dot(jnp.concatenate(pieces, axis=1), conv_w[9 * a : 9 * a + 9].reshape(2304, 256))
        acc = term if acc is None else acc + term
    sig = jax.nn.sigmoid(acc)
    cotangent = cot[...].reshape(256, 256).astype(F32)
    gp[1, 32:288] = (cotangent * (sig * (1.0 + acc * (1.0 - sig)))).astype(BF)

    grad_copies = []
    for dx, plane in ((1, 0), (-1, 2), (0, 1)):
        for dz, src, dst in ((0, whole, whole), (1, low, first), (-1, high, last)):
            if (dx, dz) != (0, 0):
                grad_copies.append(
                    send(gp.at[1, src], gp.at[plane, dst], halo_s.at[n], halo_r.at[n], at(dx, dz))
                )
                n += 1

    for copy in far_copies:
        copy.wait_recv()
    far_plane = 3 - 3 * c
    far_ok = jnp.logical_and(gx + 2 - 4 * c >= 0, gx + 2 - 4 * c < 32)
    q[far_plane, c, 32:288] = jnp.where(far_ok, q[far_plane, c, 32:288], jnp.zeros((256, 128), BF))
    for rows, ok in ((slice(0, 32), top), (slice(288, 320), bottom)):
        both = jnp.logical_and(far_ok, ok)
        q[far_plane, c, rows] = jnp.where(both, q[far_plane, c, rows], jnp.zeros((32, 128), BF))
    for plane in range(4):
        for b in range(3):
            ht[b, plane] = dot_t(eye, q[plane, c, 32 * b : 32 * b + 256]).astype(BF)

    grad_copies[0].wait_recv()
    grad_copies[3].wait_recv()
    for a, valid in ((0, left), (2, right)):
        gp[a, 32:288] = jnp.where(valid, gp[a, 32:288], jnp.zeros((256, 256), BF))
    for a in range(3):
        for i, shift in ((0, after), (1, before)):
            gs[i, a, 32:288] = dot(shift, gp[a, 32:288]).astype(BF)

    class Stream:
        def __init__(self, index):
            self.i = index
            self.t0, self.n, self.x_first = STREAMS[index]
            self.f, self.s = (px, py) if self.x_first else (py, px)
            self.first, self.second = (on_x, on_y) if self.x_first else (on_y, on_x)

        def sems(self, slot):
            return step_s.at[self.i, slot], step_r.at[self.i, slot]

        def rows(self, f):
            return pl.ds(pl.multiple_of(32 * f, 32), 32)

        def tile(self, s):
            return pl.ds(pl.multiple_of(16 * (s % 2), 16), 16), pl.ds(pl.multiple_of(128 * (s // 2), 128), 128)

        def out_rows(self, f):
            return pl.ds(pl.multiple_of(c * 128 + 32 * f, 32), 32)

        def out_tile(self):
            lanes = pl.ds(pl.multiple_of(128 * (self.s // 2), 128), 128)
            return pl.ds(pl.multiple_of(c * 128 + 32 * self.f + 16 * (self.s % 2), 16), 16), lanes

        def start_first(self):
            self.c1 = []
            for k in (1, 2, 3):
                src = sums.at[self.t0 : self.t0 + self.n, self.rows((self.f + k) % 4)]
                dst = r1.at[self.i, k - 1, 0 : self.n]
                self.c1.append(send(src, dst, *self.sems(k - 1), self.first(k)))

        def start_second(self):
            total = sums[self.t0 : self.t0 + self.n, self.rows(self.f)].astype(F32)
            for k in (1, 2, 3):
                self.c1[k - 1].wait_recv()
                total = total + r1[self.i, k - 1, 0 : self.n].astype(F32)
            y1[self.i, 0 : self.n] = total.astype(BF)
            self.c2 = []
            for k in (1, 2, 3):
                rows, lanes = self.tile((self.s + k) % 4)
                src, dst = y1.at[self.i, 0 : self.n, rows, lanes], r2.at[self.i, k - 1, 0 : self.n]
                self.c2.append(send(src, dst, *self.sems(2 + k), self.second(k)))

        def start_third(self):
            rows, lanes = self.tile(self.s)
            total = y1[self.i, 0 : self.n, rows, lanes].astype(F32)
            for k in (1, 2, 3):
                self.c2[k - 1].wait_recv()
                total = total + r2[self.i, k - 1, 0 : self.n].astype(F32)
            z1[self.i, 0 : self.n] = total.astype(BF)
            if self.n < 8:
                z1[self.i, self.n : 8] = jnp.zeros((8 - self.n, 16, 128), BF)
            self.c3 = []
            for k in range(1, 8):
                self.c3.append(send(z1.at[self.i, (z + k) % 8], r3.at[self.i, k - 1], *self.sems(5 + k), on_z(k)))

        def gather_third(self):
            total = z1[self.i, z].astype(F32)
            for k in range(1, 8):
                self.c3[k - 1].wait_recv()
                total = total + r3[self.i, k - 1].astype(F32)
            rows, lanes = self.out_tile()
            out[self.i, z, rows, lanes] = total.astype(BF)
            self.c4 = []
            here = out.at[self.i, z, rows, lanes]
            for k in range(1, 8):
                self.c4.append(send(here, here, *self.sems(12 + k), on_z(k)))

        def gather_second(self):
            for copy in self.c4:
                copy.wait_recv()
            rows, lanes = self.out_tile()
            here = out.at[self.i, 0 : self.n, rows, lanes]
            self.c5 = [send(here, here, *self.sems(19 + k), self.second(k)) for k in (1, 2, 3)]

        def gather_first(self):
            for copy in self.c5:
                copy.wait_recv()
            here = out.at[self.i, 0 : self.n, self.out_rows(self.f)]
            self.c6 = [send(here, here, *self.sems(22 + k), self.first(k)) for k in (1, 2, 3)]
            self.c7 = [send(here, here, *self.sems(26), partner)]

        def gather_core(self):
            for k in (1, 2, 3):
                self.c6[k - 1].wait_recv()
                here = out.at[self.i, 0 : self.n, self.out_rows((self.f + 4 - k) % 4)]
                self.c7.append(send(here, here, *self.sems(26 + k), partner))

        def finish(self):
            for copy in self.c7:
                copy.wait_recv()
            if self.i < CONV_STREAMS:
                dst = conv_out.at[self.t0 : self.t0 + self.n]
                src = out.at[self.i, 0 : self.n]
                self.o = pltpu.make_async_copy(src, dst, out_sem.at[self.i])
                self.o.start()

    streams = [Stream(i) for i in range(len(STREAMS))]

    def grad_rows(s, p):
        a = p + 1 - c
        return gp[a, 32:288] if s == 1 else gs[s // 2, a, 32:288]

    both_planes = [jnp.concatenate([grad_rows(s, 0), grad_rows(s, 1)], axis=0) for s in range(3)]
    for stream in streams[:CONV_STREAMS]:
        for t in range(stream.t0, stream.t0 + stream.n):
            a, b, s = t // 9, (t // 3) % 3, t % 3
            lhs = jnp.concatenate([ht[b, a], ht[b, a + 1]], axis=1)
            sums[t] = dot(lhs, both_planes[s]).astype(BF)
        stream.start_first()

    for i, copy in enumerate(grad_copies):
        if i not in (0, 3):
            copy.wait_recv()
    for a, valid in ((0, left), (1, None), (2, right)):
        for rows, ok in ((slice(0, 32), top), (slice(288, 320), bottom)):
            both = ok if valid is None else jnp.logical_and(ok, valid)
            gp[a, rows] = jnp.where(both, gp[a, rows], jnp.zeros((32, 256), BF))
            for i, shift in ((0, after), (1, before)):
                gs[i, a, rows] = dot(shift[0:32, 0:32], gp[a, rows]).astype(BF)
    back = cotangent
    for a in range(3):
        for b in range(3):
            rows = slice(32 * (2 - b), 32 * (2 - b) + 256)
            for s in range(3):
                piece = gp[2 - a, rows] if s == 1 else gs[s // 2, 2 - a, rows]
                back = back + dot_t(piece, conv_w[9 * a + 3 * b + s])
    hidden_grad = back.astype(BF)
    for t in range(4):
        part[t] = dot(x_t[4 * (1 - c) + t], hidden_grad).astype(BF)
    down_copy = send(part, part_in, halo_s.at[n], halo_r.at[n], partner)
    n += 1

    for stream in streams[:CONV_STREAMS]:
        stream.start_second()

    unsort = ones_where(row == target(col))
    for a in range(2):
        flat = [dot_t(hidden_grad, down_w[4 * a + g]).astype(BF) for g in range(4)]
        for block in range(4):
            rows = jnp.concatenate([f[64 * block : 64 * block + 64] for f in flat], axis=0)
            fine_out[a, 4 * block : 4 * block + 4] = dot(unsort, rows).astype(BF).reshape(4, 64, 128)

    for stream in streams[:CONV_STREAMS]:
        stream.start_third()

    own = [dot(x_t[4 * c + t], hidden_grad) for t in range(4)]
    down_copy.wait_recv()
    for t in range(4):
        sums[27 + t] = (own[t] + part_in[t].astype(F32)).astype(BF)
    streams[4].start_first()

    for stream in streams[:CONV_STREAMS]:
        stream.gather_third()
    streams[4].start_second()
    for stream in streams[:CONV_STREAMS]:
        stream.gather_second()
    streams[4].start_third()
    for stream in streams[:CONV_STREAMS]:
        stream.gather_first()
    streams[4].gather_third()
    streams[4].gather_second()
    for stream in streams[:CONV_STREAMS]:
        stream.gather_core()
    streams[4].gather_first()
    for stream in streams[:CONV_STREAMS]:
        stream.finish()
    streams[4].gather_core()
    streams[4].finish()
    for core in range(2):
        down_out[4 * core : 4 * core + 4] = out[4, 0:4, 128 * core : 128 * core + 128]
    for copy in started:
        copy.wait_send()
    for stream in streams[:CONV_STREAMS]:
        stream.o.wait()


def on_device(fine_field, down_weight, conv_weight, coarse_cotangent):
    vmem = pl.BlockSpec(memory_space=pltpu.VMEM)
    count = len(STREAMS)
    return pl.pallas_call(
        kernel,
        out_shape=(
            jax.ShapeDtypeStruct(fine_field.shape, BF),
            jax.ShapeDtypeStruct(conv_weight.shape, BF),
            jax.ShapeDtypeStruct(down_weight.shape, BF),
        ),
        in_specs=[vmem] * 4,
        out_specs=(vmem, pl.BlockSpec(memory_space=pl.ANY), vmem),
        scratch_shapes=[
            pltpu.VMEM((256, 1024), BF),
            pltpu.VMEM((8, 128, 256), BF),
            pltpu.VMEM((4, 2, 320, 128), BF),
            pltpu.VMEM((2, 3, 320, 256), BF),
            pltpu.VMEM((3, 4, 128, 256), BF),
            pltpu.VMEM((3, 320, 256), BF),
            pltpu.VMEM((2, 3, 320, 256), BF),
            pltpu.VMEM((31, 128, 256), BF),
            pltpu.VMEM((4, 128, 256), BF),
            pltpu.VMEM((4, 128, 256), BF),
            pltpu.VMEM((count, 3, 8, 32, 256), BF),
            pltpu.VMEM((count, 8, 32, 256), BF),
            pltpu.VMEM((count, 3, 8, 16, 128), BF),
            pltpu.VMEM((count, 8, 16, 128), BF),
            pltpu.VMEM((count, 7, 16, 128), BF),
            pltpu.VMEM((count, 8, 256, 256), BF),
            pltpu.SemaphoreType.DMA((20,)),
            pltpu.SemaphoreType.DMA((20,)),
            pltpu.SemaphoreType.DMA((count, 30)),
            pltpu.SemaphoreType.DMA((count, 30)),
            pltpu.SemaphoreType.DMA((count,)),
        ],
        compiler_params=pltpu.CompilerParams(
            collective_id=0, has_side_effects=True, vmem_limit_bytes=48 * 1024 * 1024
        ),
        name="section_backward",
    )(fine_field, down_weight, conv_weight, coarse_cotangent)


def solution(mesh):
    in_specs = (P("gx", "gy", None, None), P(), P(), P("gx", "gy", None, None))
    out_specs = (P("gx", "gy", None, None), P(), P())
    return jax.shard_map(
        on_device, mesh=mesh, in_specs=in_specs, out_specs=out_specs, check_vma=False
    )
```

```python
import jax
import jax.numpy as jnp
from jax import lax
from jax.experimental import pallas as pl
from jax.experimental.pallas import tpu as pltpu
from jax.sharding import PartitionSpec as P

MESH = pl.DeviceIdType.MESH
BF = jnp.bfloat16
F32 = jnp.float32

STREAMS = ((0, 7, True), (7, 7, False), (14, 7, True), (21, 6, False), (27, 4, True))
CONV_STREAMS = 4


def dot(a, b):
    return jnp.dot(a, b, preferred_element_type=F32)


def dot_t(a, b):
    return lax.dot_general(a, b, (((1,), (1,)), ((), ())), preferred_element_type=F32)


def iotas(n):
    return lax.broadcasted_iota(jnp.int32, (n, n), 0), lax.broadcasted_iota(jnp.int32, (n, n), 1)


def ones_where(mask):
    return jnp.where(mask, 1.0, 0.0).astype(BF)


def kernel(
    fine_in, down_in, conv_in, cot_in, fine_out, conv_out, down_out,
    fine, down_w, conv_w, cot, x_mat, x_t, q, hs, ht, gp, gs, sums, part, part_in, r1, y1, r2, z1, r3, out,
    halo_s, halo_r, step_s, step_r, out_sem, in_sem,
):
    gx, z = lax.axis_index("gx"), lax.axis_index("gy")
    px, py, c = gx // 8, (gx // 2) % 4, gx % 2

    def at(dx, dz):
        return ((gx + dx + 32) % 32, (z + dz + 8) % 8)

    def on_x(k):
        return ((((px + k) % 4) * 4 + py) * 2 + c, z)

    def on_y(k):
        return ((px * 4 + (py + k) % 4) * 2 + c, z)

    def on_z(k):
        return (gx, (z + k) % 8)

    partner = (gx + 1 - 2 * c, z)
    other = 2 * c - 1

    loads = []
    for i, (src, dst) in enumerate(((fine_in, fine), (down_in, down_w), (cot_in, cot), (conv_in, conv_w))):
        load = pltpu.make_async_copy(src, dst, in_sem.at[i])
        load.start()
        loads.append(load)

    greeted = [at(dx, dz) for dx in (-1, 0, 1) for dz in (-1, 0, 1) if (dx, dz) != (0, 0)]
    greeted += [on_x(k) for k in (1, 2, 3)] + [on_y(k) for k in (1, 2, 3)]
    greeted += [on_z(k) for k in range(2, 7)]
    barrier = pltpu.get_barrier_semaphore()
    for device in greeted:
        pl.semaphore_signal(barrier, inc=1, device_id=device, device_id_type=MESH)

    started = []

    def send(src, dst, s_sem, r_sem, device):
        copy = pltpu.make_async_remote_copy(
            src_ref=src, dst_ref=dst, send_sem=s_sem, recv_sem=r_sem, device_id=device, device_id_type=MESH
        )
        copy.start()
        started.append(copy)
        return copy

    row, col = iotas(256)

    def target(r):
        group, j, k = r >> 6, (r >> 5) & 1, r & 31
        return (j * 2 + (group >> 1)) * 64 + 2 * k + (group & 1)

    sort = ones_where(col == target(row))
    before = ones_where((col == row - 1) & ((row & 31) != 0))
    after = ones_where((col == row + 1) & ((row & 31) != 31))
    r128, c128 = iotas(128)
    eye = ones_where(r128 == c128)
    loads[0].wait()
    loads[1].wait()
    for a in range(2):
        for block in range(4):
            rows = fine[a, 4 * block : 4 * block + 4].reshape(256, 128)
            sorted_rows = dot(sort, rows).astype(BF)
            for group in range(4):
                lane = (4 * a + group) * 128
                x_mat[64 * block : 64 * block + 64, lane : lane + 128] = sorted_rows[64 * group : 64 * group + 64]
    hidden = dot(x_mat[...], down_w[...].reshape(1024, 256)).astype(BF)
    mine = 1 + c
    for half in range(2):
        q[mine, half, 32:288, :] = hidden[:, 128 * half : 128 * half + 128]

    pl.semaphore_wait(barrier, len(greeted))

    whole, low, high = pl.ds(32, 256), pl.ds(256, 32), pl.ds(32, 32)
    first, last = pl.ds(0, 32), pl.ds(288, 32)
    sides = ((-other, 1 + c, 2 * c), (other, 3 * (1 - c), 2 - 2 * c), (0, 1 + c, 1))
    shifts = ((0, whole, whole), (1, low, first), (-1, high, last))
    n = 0

    def halo(source_of, target_of):
        nonlocal n
        copies = []
        for dz, src, dst in shifts:
            for side in range(3):
                if (dz, side) != (0, 2):
                    dx = sides[side][0]
                    sent = send(source_of(src), target_of(side, dst), halo_s.at[n], halo_r.at[n], at(dx, dz))
                    copies.append(sent)
                    n += 1
        return copies

    hidden_copies = halo(lambda rows: q.at[mine, :, rows], lambda side, rows: q.at[sides[side][1], :, rows])
    for t in range(8):
        x_t[t] = dot_t(eye, x_mat[:, 128 * t : 128 * t + 128]).astype(BF)

    for copy in hidden_copies:
        copy.wait_recv()
    top, bottom = z > 0, z < 7
    other_ok = jnp.logical_and(gx + other >= 0, gx + other < 32)
    far_plane = 3 * c
    q[far_plane, :, 32:288] = jnp.where(other_ok, q[far_plane, :, 32:288], jnp.zeros((2, 256, 128), BF))
    edges = ((slice(0, 32), top), (slice(288, 320), bottom))
    for plane, valid in ((1, None), (2, None), (far_plane, other_ok)):
        for rows, ok in edges:
            both = ok if valid is None else jnp.logical_and(ok, valid)
            q[plane, :, rows] = jnp.where(both, q[plane, :, rows], jnp.zeros((2, 32, 128), BF))
    beyond = q.at[far_plane, 1 - c]
    far_copy = send(beyond, beyond, halo_s.at[n], halo_r.at[n], partner)
    n += 1
    loads[3].wait()
    acc = None
    for a in range(3):
        plane = jnp.concatenate([q[c + a, 0], q[c + a, 1]], axis=1)
        for i, shift in ((0, before), (1, after)):
            hs[i, a, 0:256] = dot(shift, plane[0:256]).astype(BF)
            hs[i, a, 256:320] = dot(shift[0:64, 0:64], plane[256:320]).astype(BF)
        pieces = []
        for b in range(3):
            rows = slice(32 * b, 32 * b + 256)
            pieces += [hs[0, a, rows], plane[rows], hs[1, a, rows]]
        term = dot(jnp.concatenate(pieces, axis=1), conv_w[9 * a : 9 * a + 9].reshape(2304, 256))
        acc = term if acc is None else acc + term
    sig = jax.nn.sigmoid(acc)
    loads[2].wait()
    cotangent = cot[...].reshape(256, 256).astype(F32)
    gp[1, 32:288] = (cotangent * (sig * (1.0 + acc * (1.0 - sig)))).astype(BF)

    grad_copies = halo(lambda rows: gp.at[1, rows], lambda side, rows: gp.at[sides[side][2], rows])
    far_copy.wait_recv()
    for plane in range(4):
        for b in range(3):
            ht[b, plane] = dot_t(eye, q[plane, c, 32 * b : 32 * b + 256]).astype(BF)
    for i, shift in ((0, after), (1, before)):
        gs[i, 1, 32:288] = dot(shift, gp[1, 32:288]).astype(BF)

    grad_copies[0].wait_recv()
    near = 2 - 2 * c
    for i, shift in ((0, after), (1, before)):
        gs[i, near, 32:288] = dot(shift, gp[near, 32:288]).astype(BF)

    class Stream:
        def __init__(self, index):
            self.i = index
            self.t0, self.n, self.x_first = STREAMS[index]
            self.f, self.s = (px, py) if self.x_first else (py, px)
            self.first, self.second = (on_x, on_y) if self.x_first else (on_y, on_x)

        def sems(self, slot):
            return step_s.at[self.i, slot], step_r.at[self.i, slot]

        def rows(self, f):
            return pl.ds(pl.multiple_of(32 * f, 32), 32)

        def tile(self, s):
            return pl.ds(pl.multiple_of(16 * (s % 2), 16), 16), pl.ds(pl.multiple_of(128 * (s // 2), 128), 128)

        def out_rows(self, f):
            return pl.ds(pl.multiple_of(c * 128 + 32 * f, 32), 32)

        def out_tile(self):
            lanes = pl.ds(pl.multiple_of(128 * (self.s // 2), 128), 128)
            return pl.ds(pl.multiple_of(c * 128 + 32 * self.f + 16 * (self.s % 2), 16), 16), lanes

        def start_first(self):
            self.c1 = []
            for k in (1, 2, 3):
                src = sums.at[self.t0 : self.t0 + self.n, self.rows((self.f + k) % 4)]
                dst = r1.at[self.i, k - 1, 0 : self.n]
                self.c1.append(send(src, dst, *self.sems(k - 1), self.first(k)))

        def start_second(self):
            total = sums[self.t0 : self.t0 + self.n, self.rows(self.f)].astype(F32)
            for k in (1, 2, 3):
                self.c1[k - 1].wait_recv()
                total = total + r1[self.i, k - 1, 0 : self.n].astype(F32)
            y1[self.i, 0 : self.n] = total.astype(BF)
            self.c2 = []
            for k in (1, 2, 3):
                rows, lanes = self.tile((self.s + k) % 4)
                src, dst = y1.at[self.i, 0 : self.n, rows, lanes], r2.at[self.i, k - 1, 0 : self.n]
                self.c2.append(send(src, dst, *self.sems(2 + k), self.second(k)))

        def start_third(self):
            rows, lanes = self.tile(self.s)
            total = y1[self.i, 0 : self.n, rows, lanes].astype(F32)
            for k in (1, 2, 3):
                self.c2[k - 1].wait_recv()
                total = total + r2[self.i, k - 1, 0 : self.n].astype(F32)
            z1[self.i, 0 : self.n] = total.astype(BF)
            if self.n < 8:
                z1[self.i, self.n : 8] = jnp.zeros((8 - self.n, 16, 128), BF)
            self.c3 = []
            for k in range(1, 8):
                self.c3.append(send(z1.at[self.i, (z + k) % 8], r3.at[self.i, k - 1], *self.sems(5 + k), on_z(k)))

        def gather_third(self):
            total = z1[self.i, z].astype(F32)
            for k in range(1, 8):
                self.c3[k - 1].wait_recv()
                total = total + r3[self.i, k - 1].astype(F32)
            rows, lanes = self.out_tile()
            out[self.i, z, rows, lanes] = total.astype(BF)
            self.c4 = []
            here = out.at[self.i, z, rows, lanes]
            for k in range(1, 8):
                self.c4.append(send(here, here, *self.sems(12 + k), on_z(k)))

        def gather_second(self):
            for copy in self.c4:
                copy.wait_recv()
            rows, lanes = self.out_tile()
            here = out.at[self.i, 0 : self.n, rows, lanes]
            self.c5 = [send(here, here, *self.sems(19 + k), self.second(k)) for k in (1, 2, 3)]

        def gather_first(self):
            for copy in self.c5:
                copy.wait_recv()
            here = out.at[self.i, 0 : self.n, self.out_rows(self.f)]
            self.c6 = [send(here, here, *self.sems(22 + k), self.first(k)) for k in (1, 2, 3)]
            self.c7 = [send(here, here, *self.sems(26), partner)]

        def gather_core(self):
            for k in (1, 2, 3):
                self.c6[k - 1].wait_recv()
                here = out.at[self.i, 0 : self.n, self.out_rows((self.f + 4 - k) % 4)]
                self.c7.append(send(here, here, *self.sems(26 + k), partner))

        def finish(self):
            for copy in self.c7:
                copy.wait_recv()
            if self.i < CONV_STREAMS:
                dst = conv_out.at[self.t0 : self.t0 + self.n]
                src = out.at[self.i, 0 : self.n]
                self.o = pltpu.make_async_copy(src, dst, out_sem.at[self.i])
                self.o.start()

    streams = [Stream(i) for i in range(len(STREAMS))]

    def grad_rows(s, p):
        a = p + 1 - c
        return gp[a, 32:288] if s == 1 else gs[s // 2, a, 32:288]

    both_planes = [jnp.concatenate([grad_rows(s, 0), grad_rows(s, 1)], axis=0) for s in range(3)]
    for stream in streams[:CONV_STREAMS]:
        for t in range(stream.t0, stream.t0 + stream.n):
            a, b, s = t // 9, (t // 3) % 3, t % 3
            lhs = jnp.concatenate([ht[b, a], ht[b, a + 1]], axis=1)
            sums[t] = dot(lhs, both_planes[s]).astype(BF)
        stream.start_first()

    for copy in grad_copies[1:]:
        copy.wait_recv()
    away = 2 * c
    gp[away, 32:288] = jnp.where(other_ok, gp[away, 32:288], jnp.zeros((256, 256), BF))
    for i, shift in ((0, after), (1, before)):
        gs[i, away, 32:288] = dot(shift, gp[away, 32:288]).astype(BF)
    for plane, valid in ((1, None), (near, None), (away, other_ok)):
        for rows, ok in edges:
            both = ok if valid is None else jnp.logical_and(ok, valid)
            gp[plane, rows] = jnp.where(both, gp[plane, rows], jnp.zeros((32, 256), BF))
            for i, shift in ((0, after), (1, before)):
                gs[i, plane, rows] = dot(shift[0:32, 0:32], gp[plane, rows]).astype(BF)
    back = cotangent
    for a in range(3):
        for b in range(3):
            rows = slice(32 * (2 - b), 32 * (2 - b) + 256)
            for s in range(3):
                piece = gp[2 - a, rows] if s == 1 else gs[s // 2, 2 - a, rows]
                back = back + dot_t(piece, conv_w[9 * a + 3 * b + s])
    hidden_grad = back.astype(BF)
    for t in range(4):
        part[t] = dot(x_t[4 * (1 - c) + t], hidden_grad).astype(BF)
    down_copy = send(part, part_in, halo_s.at[n], halo_r.at[n], partner)
    n += 1

    for stream in streams[:CONV_STREAMS]:
        stream.start_second()

    unsort = ones_where(row == target(col))
    for a in range(2):
        flat = [dot_t(hidden_grad, down_w[4 * a + g]).astype(BF) for g in range(4)]
        for block in range(4):
            rows = jnp.concatenate([f[64 * block : 64 * block + 64] for f in flat], axis=0)
            fine_out[a, 4 * block : 4 * block + 4] = dot(unsort, rows).astype(BF).reshape(4, 64, 128)

    for stream in streams[:CONV_STREAMS]:
        stream.start_third()

    own = [dot(x_t[4 * c + t], hidden_grad) for t in range(4)]
    down_copy.wait_recv()
    for t in range(4):
        sums[27 + t] = (own[t] + part_in[t].astype(F32)).astype(BF)
    streams[4].start_first()

    for stream in streams[:CONV_STREAMS]:
        stream.gather_third()
    streams[4].start_second()
    for stream in streams[:CONV_STREAMS]:
        stream.gather_second()
    streams[4].start_third()
    for stream in streams[:CONV_STREAMS]:
        stream.gather_first()
    streams[4].gather_third()
    streams[4].gather_second()
    for stream in streams[:CONV_STREAMS]:
        stream.gather_core()
    streams[4].gather_first()
    for stream in streams[:CONV_STREAMS]:
        stream.finish()
    streams[4].gather_core()
    streams[4].finish()
    for core in range(2):
        down_out[4 * core : 4 * core + 4] = out[4, 0:4, 128 * core : 128 * core + 128]
    for copy in started:
        copy.wait_send()
    for stream in streams[:CONV_STREAMS]:
        stream.o.wait()


def deliver(fine, conv, down, fine_out, conv_out, down_out, sems):
    copies = []
    for i, (src, dst) in enumerate(((conv, conv_out), (fine, fine_out), (down, down_out))):
        copy = pltpu.make_async_copy(src, dst, sems.at[i])
        copy.start()
        copies.append(copy)
    for copy in copies:
        copy.wait()


def on_device(fine_field, down_weight, conv_weight, coarse_cotangent):
    vmem = pl.BlockSpec(memory_space=pltpu.VMEM)
    count = len(STREAMS)
    operands = (fine_field, down_weight, conv_weight, coarse_cotangent)
    operands = [pltpu.with_memory_space_constraint(x, pltpu.HBM) for x in operands]
    results = pl.pallas_call(
        kernel,
        out_shape=(
            jax.ShapeDtypeStruct(fine_field.shape, BF),
            jax.ShapeDtypeStruct(conv_weight.shape, BF),
            jax.ShapeDtypeStruct(down_weight.shape, BF),
        ),
        in_specs=[pl.BlockSpec(memory_space=pltpu.HBM)] * 4,
        out_specs=(vmem, pl.BlockSpec(memory_space=pl.ANY), vmem),
        scratch_shapes=[
            pltpu.VMEM(fine_field.shape, BF),
            pltpu.VMEM(down_weight.shape, BF),
            pltpu.VMEM(conv_weight.shape, BF),
            pltpu.VMEM(coarse_cotangent.shape, BF),
            pltpu.VMEM((256, 1024), BF),
            pltpu.VMEM((8, 128, 256), BF),
            pltpu.VMEM((4, 2, 320, 128), BF),
            pltpu.VMEM((2, 3, 320, 256), BF),
            pltpu.VMEM((3, 4, 128, 256), BF),
            pltpu.VMEM((3, 320, 256), BF),
            pltpu.VMEM((2, 3, 320, 256), BF),
            pltpu.VMEM((31, 128, 256), BF),
            pltpu.VMEM((4, 128, 256), BF),
            pltpu.VMEM((4, 128, 256), BF),
            pltpu.VMEM((count, 3, 8, 32, 256), BF),
            pltpu.VMEM((count, 8, 32, 256), BF),
            pltpu.VMEM((count, 3, 8, 16, 128), BF),
            pltpu.VMEM((count, 8, 16, 128), BF),
            pltpu.VMEM((count, 7, 16, 128), BF),
            pltpu.VMEM((count, 8, 256, 256), BF),
            pltpu.SemaphoreType.DMA((20,)),
            pltpu.SemaphoreType.DMA((20,)),
            pltpu.SemaphoreType.DMA((count, 30)),
            pltpu.SemaphoreType.DMA((count, 30)),
            pltpu.SemaphoreType.DMA((count,)),
            pltpu.SemaphoreType.DMA((4,)),
        ],
        compiler_params=pltpu.CompilerParams(
            collective_id=0, has_side_effects=True, vmem_limit_bytes=36 * 1024 * 1024
        ),
        name="section_backward",
    )(*operands)
    hbm = pl.BlockSpec(memory_space=pltpu.HBM)
    return pl.pallas_call(
        deliver,
        out_shape=tuple(jax.ShapeDtypeStruct(r.shape, r.dtype) for r in results),
        in_specs=[vmem] * 3,
        out_specs=(hbm, hbm, hbm),
        scratch_shapes=[pltpu.SemaphoreType.DMA((3,))],
        compiler_params=pltpu.CompilerParams(vmem_limit_bytes=1024 * 1024),
        name="deliver",
    )(*[pltpu.with_memory_space_constraint(r, pltpu.VMEM) for r in results])


def solution(mesh):
    in_specs = (P("gx", "gy", None, None), P(), P(), P("gx", "gy", None, None))
    out_specs = (P("gx", "gy", None, None), P(), P())
    return jax.shard_map(
        on_device, mesh=mesh, in_specs=in_specs, out_specs=out_specs, check_vma=False
    )
```

```python
import math

import jax
import jax.numpy as jnp
from jax import lax
from jax.experimental import pallas as pl
from jax.experimental.pallas import tpu as pltpu
from jax.sharding import PartitionSpec as P

MESH = pl.DeviceIdType.MESH
BF = jnp.bfloat16
F32 = jnp.float32

GROUPS = (((0, 4), (4, 4)), ((8, 4), (12, 4)), ((16, 4), (20, 4)), ((24, 3), (27, 4)))
CONV_TAPS = 27
SEMAPHORES = 54


def dot(a, b):
    return jnp.dot(a, b, preferred_element_type=F32)


def dot_t(a, b):
    return lax.dot_general(a, b, (((1,), (1,)), ((), ())), preferred_element_type=F32)


def iotas(n):
    return lax.broadcasted_iota(jnp.int32, (n, n), 0), lax.broadcasted_iota(jnp.int32, (n, n), 1)


def ones_where(mask):
    return jnp.where(mask, 1.0, 0.0).astype(BF)


def kernel(
    fine_in, down_in, conv_in, cot_in, fine_out, out,
    fine, down_w, conv_w, cot, x_mat, x_t, q, hs, ht, gp, gs, sums, part, part_in, r1, y1, r2, z1, r3, measure, sems,
):
    gx, z = lax.axis_index("gx"), lax.axis_index("gy")
    px, py, c = gx // 8, (gx // 2) % 4, gx % 2

    def at(dx, dz):
        return ((gx + dx + 32) % 32, (z + dz + 8) % 8)

    def on_x(k):
        return ((((px + k) % 4) * 4 + py) * 2 + c, z)

    def on_y(k):
        return ((px * 4 + (py + k) % 4) * 2 + c, z)

    def on_z(k):
        return (gx, (z + k) % 8)

    partner = (gx + 1 - 2 * c, z)
    other = 2 * c - 1

    names, amounts = {}, {}

    def sem(name):
        return sems.at[names.setdefault(name, len(names))]

    def count(name, ref):
        amounts[name] = amounts.get(name, 0) + math.prod(ref.shape) // 2048

    def wait(name):
        tiles = measure.at[0 : amounts.pop(name)]
        pltpu.make_async_copy(tiles, tiles, sem(name)).wait()

    def wait_all():
        for name in list(amounts):
            wait(name)

    def load(src, dst, name):
        count(name, src)
        pltpu.make_async_copy(src, dst, sem(name)).start()

    def send(src, dst, sent, received, device):
        count(sent, src)
        count(received, src)
        pltpu.make_async_remote_copy(
            src_ref=src, dst_ref=dst, send_sem=sem(sent), recv_sem=sem(received), device_id=device, device_id_type=MESH
        ).start()

    load(fine_in, fine, "fine")
    load(down_in, down_w, "fine")
    load(cot_in, cot, "cot")
    load(conv_in, conv_w, "conv")

    greeted = [at(dx, dz) for dx in (-1, 0, 1) for dz in (-1, 0, 1) if (dx, dz) != (0, 0)]
    greeted += [on_x(k) for k in (1, 2, 3)] + [on_y(k) for k in (1, 2, 3)]
    greeted += [on_z(k) for k in range(2, 7)]
    barrier = pltpu.get_barrier_semaphore()
    for device in greeted:
        pl.semaphore_signal(barrier, inc=1, device_id=device, device_id_type=MESH)

    row, col = iotas(256)

    def target(r):
        group, j, k = r >> 6, (r >> 5) & 1, r & 31
        return (j * 2 + (group >> 1)) * 64 + 2 * k + (group & 1)

    sort = ones_where(col == target(row))
    before = ones_where((col == row - 1) & ((row & 31) != 0))
    after = ones_where((col == row + 1) & ((row & 31) != 31))
    r128, c128 = iotas(128)
    eye = ones_where(r128 == c128)
    wait("fine")
    for a in range(2):
        for block in range(4):
            rows = fine[a, 4 * block : 4 * block + 4].reshape(256, 128)
            sorted_rows = dot(sort, rows).astype(BF)
            for group in range(4):
                lane = (4 * a + group) * 128
                x_mat[64 * block : 64 * block + 64, lane : lane + 128] = sorted_rows[64 * group : 64 * group + 64]
    hidden = dot(x_mat[...], down_w[...].reshape(1024, 256)).astype(BF)
    mine = 1 + c
    for half in range(2):
        q[mine, half, 32:288, :] = hidden[:, 128 * half : 128 * half + 128]

    pl.semaphore_wait(barrier, len(greeted))

    whole, low, high = pl.ds(32, 256), pl.ds(256, 32), pl.ds(32, 32)
    first, last = pl.ds(0, 32), pl.ds(288, 32)
    sides = ((-other, 1 + c, 2 * c), (other, 3 * (1 - c), 2 - 2 * c), (0, 1 + c, 1))
    shifts = ((0, whole, whole), (1, low, first), (-1, high, last))

    def halo(kind, source_of, target_of):
        for dz, src, dst in shifts[1:] + shifts[:1]:
            for side in (2, 0, 1):
                if (dz, side) != (0, 2):
                    name = (kind, side, dz == 0 and kind == "grad")
                    send(source_of(src), target_of(side, dst), "halo sent", name, at(sides[side][0], dz))

    halo("hidden", lambda rows: q.at[mine, :, rows], lambda side, rows: q.at[sides[side][1], :, rows])
    for t in range(8):
        x_t[t] = dot_t(eye, x_mat[:, 128 * t : 128 * t + 128]).astype(BF)

    top, bottom = z > 0, z < 7
    other_ok = jnp.logical_and(gx + other >= 0, gx + other < 32)
    far_plane = 3 * c
    edges = ((slice(0, 32), top), (slice(288, 320), bottom))

    def clear(ref, index, rows, ok):
        old = ref[index + (rows,)]
        ref[index + (rows,)] = jnp.where(ok, old, jnp.zeros(old.shape, BF))

    acc = None
    for role, plane, a, side in ((0, mine, 1, 2), (1, 2 - c, 2 - 2 * c, 0), (2, far_plane, 2 * c, 1)):
        wait(("hidden", side, False))
        for rows, ok in edges:
            clear(q, (plane, slice(None)), rows, ok if side != 1 else jnp.logical_and(ok, other_ok))
        if side == 1:
            clear(q, (plane, slice(None)), slice(32, 288), other_ok)
            beyond = q.at[far_plane, 1 - c]
            send(beyond, beyond, "halo sent", "far", partner)
        elif side == 2:
            wait("conv")
        rows_of = jnp.concatenate([q[plane, 0], q[plane, 1]], axis=1)
        for i, shift in ((0, before), (1, after)):
            hs[i, role, 0:256] = dot(shift, rows_of[0:256]).astype(BF)
            hs[i, role, 256:320] = dot(shift[0:64, 0:64], rows_of[256:320]).astype(BF)
        pieces = []
        for b in range(3):
            rows = slice(32 * b, 32 * b + 256)
            pieces += [hs[0, role, rows], rows_of[rows], hs[1, role, rows]]
        taps = conv_w[pl.ds(9 * a, 9)].reshape(2304, 256)
        term = dot(jnp.concatenate(pieces, axis=1), taps)
        acc = term if acc is None else acc + term
    sig = jax.nn.sigmoid(acc)
    wait("cot")
    cotangent = cot[...].reshape(256, 256).astype(F32)
    gp[1, 32:288] = (cotangent * (sig * (1.0 + acc * (1.0 - sig)))).astype(BF)

    halo("grad", lambda rows: gp.at[1, rows], lambda side, rows: gp.at[sides[side][2], rows])
    wait("far")
    for plane in range(4):
        for b in range(3):
            ht[b, plane] = dot_t(eye, q[plane, c, 32 * b : 32 * b + 256]).astype(BF)
    for i, shift in ((0, after), (1, before)):
        gs[i, 1, 32:288] = dot(shift, gp[1, 32:288]).astype(BF)

    wait(("grad", 0, True))
    near = 2 - 2 * c
    for i, shift in ((0, after), (1, before)):
        gs[i, near, 32:288] = dot(shift, gp[near, 32:288]).astype(BF)

    def row_block(f):
        return pl.ds(pl.multiple_of(32 * f, 32), 32)

    class Stream:
        def __init__(self, group, half):
            self.i, self.group = 2 * group + half, group
            self.t0, self.n = GROUPS[group][half]
            self.tile0 = self.t0 - 8 * group
            self.f, self.s = (px, py) if half == 0 else (py, px)
            self.first, self.second = (on_x, on_y) if half == 0 else (on_y, on_x)
            self.row = c * 128 + 32 * self.f + 16 * (self.s % 2)
            self.lane = 128 * (self.s // 2)

        def send(self, src, dst, name, device):
            send(src, dst, ("sent", self.group), (name, self.group), device)

        def tile(self, s):
            return pl.ds(pl.multiple_of(16 * (s % 2), 16), 16), pl.ds(pl.multiple_of(128 * (s // 2), 128), 128)

        def out_rows(self, f):
            rows = pl.ds(pl.multiple_of(c * 128 + 32 * f, 32), 32)
            return out.at[self.t0 : self.t0 + self.n, rows]

        def start_first(self):
            for k in (1, 3, 2):
                src = sums.at[self.t0 : self.t0 + self.n, row_block((self.f + k) % 4)]
                self.send(src, r1.at[self.i, k - 1, 0 : self.n], "first", self.first(k))

        def start_second(self):
            total = sums[self.t0 : self.t0 + self.n, row_block(self.f)].astype(F32)
            for k in range(3):
                total = total + r1[self.i, k, 0 : self.n].astype(F32)
            y1[self.i, 0 : self.n] = total.astype(BF)
            for k in (1, 3, 2):
                rows, lanes = self.tile((self.s + k) % 4)
                src = y1.at[self.i, 0 : self.n, rows, lanes]
                self.send(src, r2.at[self.i, k - 1, 0 : self.n], "second", self.second(k))

        def sum_second(self):
            rows, lanes = self.tile(self.s)
            total = y1[self.i, 0 : self.n, rows, lanes].astype(F32)
            for k in range(3):
                total = total + r2[self.i, k, 0 : self.n].astype(F32)
            z1[self.group, self.tile0 : self.tile0 + self.n] = total.astype(BF)

        def gather_second(self):
            rows = pl.ds(pl.multiple_of(self.row, 16), 16)
            lanes = pl.ds(pl.multiple_of(self.lane, 128), 128)
            here = out.at[self.t0 : self.t0 + self.n, rows, lanes]
            for k in (1, 3, 2):
                self.send(here, here, "gather second", self.second(k))

        def gather_first(self):
            here = self.out_rows(self.f)
            for k in (1, 3, 2):
                self.send(here, here, ("gather first", k), self.first(k))
            self.send(here, here, "core", partner)

        def gather_core(self, k):
            here = self.out_rows((self.f + 4 - k) % 4)
            self.send(here, here, "core", partner)

    class Group:
        def __init__(self, index):
            self.i = index
            self.streams = [Stream(index, half) for half in range(2)]

        def send(self, src, dst, name, device):
            send(src, dst, ("sent", self.i), (name, self.i), device)

        def start_first(self):
            for stream in self.streams:
                stream.start_first()

        def start_second(self):
            wait(("first", self.i))
            for stream in self.streams:
                stream.start_second()

        def start_third(self):
            wait(("second", self.i))
            for stream in self.streams:
                stream.sum_second()
            end = self.streams[1].tile0 + self.streams[1].n
            if end < 8:
                z1[self.i, end:8] = jnp.zeros((8 - end, 16, 128), BF)
            for k in (4, 3, 5, 2, 6, 1, 7):
                self.send(z1.at[self.i, (z + k) % 8], r3.at[self.i, k - 1], "third", on_z(k))

        def gather_third(self):
            wait(("third", self.i))
            total = z1[self.i, z].astype(F32)
            for k in range(7):
                total = total + r3[self.i, k].astype(F32)
            a, b = self.streams
            later = (z + 8 - b.tile0) // 8
            rows = pl.ds(pl.multiple_of(a.row + later * (b.row - a.row), 16), 16)
            lanes = pl.ds(pl.multiple_of(a.lane + later * (b.lane - a.lane), 128), 128)
            out[8 * self.i + z, rows, lanes] = total.astype(BF)
            here = out.at[8 * self.i + z, rows, lanes]
            for k in (4, 3, 5, 2, 6, 1, 7):
                self.send(here, here, "gather third", on_z(k))

        def gather_second(self):
            wait(("gather third", self.i))
            for stream in self.streams:
                stream.gather_second()

        def gather_first(self):
            wait(("gather second", self.i))
            for stream in self.streams:
                stream.gather_first()

        def gather_core(self):
            for k in (1, 3, 2):
                wait((("gather first", k), self.i))
                for stream in self.streams:
                    stream.gather_core(k)

        def finish(self):
            wait(("core", self.i))

    groups = [Group(i) for i in range(len(GROUPS))]

    def grad_rows(s, p):
        a = p + 1 - c
        return gp[a, 32:288] if s == 1 else gs[s // 2, a, 32:288]

    both_planes = [jnp.concatenate([grad_rows(s, 0), grad_rows(s, 1)], axis=0) for s in range(3)]
    for t in range(CONV_TAPS):
        a, b, s = t // 9, (t // 3) % 3, t % 3
        lhs = jnp.concatenate([ht[b, a], ht[b, a + 1]], axis=1)
        sums[t] = dot(lhs, both_planes[s]).astype(BF)
        if t % 8 == 7:
            groups[t // 8].start_first()

    for name in (("grad", 2, False), ("grad", 0, False), ("grad", 1, False), ("grad", 1, True)):
        wait(name)
    away = 2 * c
    clear(gp, (away,), slice(32, 288), other_ok)
    for i, shift in ((0, after), (1, before)):
        gs[i, away, 32:288] = dot(shift, gp[away, 32:288]).astype(BF)
    for plane, valid in ((1, None), (near, None), (away, other_ok)):
        for rows, ok in edges:
            clear(gp, (plane,), rows, ok if valid is None else jnp.logical_and(ok, valid))
            for i, shift in ((0, after), (1, before)):
                gs[i, plane, rows] = dot(shift[0:32, 0:32], gp[plane, rows]).astype(BF)
    back = cotangent
    for a in range(3):
        for b in range(3):
            rows = slice(32 * (2 - b), 32 * (2 - b) + 256)
            for s in range(3):
                piece = gp[2 - a, rows] if s == 1 else gs[s // 2, 2 - a, rows]
                back = back + dot_t(piece, conv_w[9 * a + 3 * b + s])
    hidden_grad = back.astype(BF)
    for t in range(4):
        part[t] = dot(x_t[4 * (1 - c) + t], hidden_grad).astype(BF)
    send(part, part_in, "halo sent", "part", partner)

    unsort = ones_where(row == target(col))

    def write_fine(a):
        flat = [dot_t(hidden_grad, down_w[4 * a + g]).astype(BF) for g in range(4)]
        for block in range(4):
            rows = jnp.concatenate([f[64 * block : 64 * block + 64] for f in flat], axis=0)
            fine_out[a, 4 * block : 4 * block + 4] = dot(unsort, rows).astype(BF).reshape(4, 64, 128)

    groups[0].start_second()
    write_fine(0)
    groups[1].start_second()
    own = [dot(x_t[4 * c + t], hidden_grad) for t in range(4)]
    wait("part")
    for t in range(4):
        sums[27 + t] = (own[t] + part_in[t].astype(F32)).astype(BF)
    groups[3].start_first()
    write_fine(1)
    groups[2].start_second()
    groups[0].start_third()
    groups[1].start_third()
    groups[3].start_second()
    groups[2].start_third()
    groups[0].gather_third()
    groups[1].gather_third()
    groups[3].start_third()
    groups[2].gather_third()
    groups[0].gather_second()
    groups[1].gather_second()
    groups[3].gather_third()
    groups[0].gather_first()
    groups[2].gather_second()
    groups[1].gather_first()
    groups[3].gather_second()
    groups[2].gather_first()
    groups[0].gather_core()
    groups[3].gather_first()
    groups[1].gather_core()
    groups[2].gather_core()
    groups[3].gather_core()
    for group in groups:
        group.finish()
    wait_all()


def deliver(fine, sums, fine_out, conv_out, down_out, sems):
    moves = [(sums.at[t : t + 9], conv_out.at[t : t + 9]) for t in range(0, CONV_TAPS, 9)]
    moves.append((fine, fine_out))
    for core in range(2):
        taps = sums.at[CONV_TAPS : CONV_TAPS + 4, 128 * core : 128 * core + 128]
        moves.append((taps, down_out.at[4 * core : 4 * core + 4]))
    copies = []
    for i, (src, dst) in enumerate(moves):
        copy = pltpu.make_async_copy(src, dst, sems.at[i])
        copy.start()
        copies.append(copy)
    for copy in copies:
        copy.wait()


def on_device(fine_field, down_weight, conv_weight, coarse_cotangent):
    vmem = pl.BlockSpec(memory_space=pltpu.VMEM)
    groups, streams = len(GROUPS), 2 * len(GROUPS)
    operands = (fine_field, down_weight, conv_weight, coarse_cotangent)
    operands = [pltpu.with_memory_space_constraint(x, pltpu.HBM) for x in operands]
    results = pl.pallas_call(
        kernel,
        out_shape=(
            jax.ShapeDtypeStruct(fine_field.shape, BF),
            jax.ShapeDtypeStruct((32, 256, 256), BF),
        ),
        in_specs=[pl.BlockSpec(memory_space=pltpu.HBM)] * 4,
        out_specs=(vmem, vmem),
        scratch_shapes=[
            pltpu.VMEM(fine_field.shape, BF),
            pltpu.VMEM(down_weight.shape, BF),
            pltpu.VMEM(conv_weight.shape, BF),
            pltpu.VMEM(coarse_cotangent.shape, BF),
            pltpu.VMEM((256, 1024), BF),
            pltpu.VMEM((8, 128, 256), BF),
            pltpu.VMEM((4, 2, 320, 128), BF),
            pltpu.VMEM((2, 3, 320, 256), BF),
            pltpu.VMEM((3, 4, 128, 256), BF),
            pltpu.VMEM((3, 320, 256), BF),
            pltpu.VMEM((2, 3, 320, 256), BF),
            pltpu.VMEM((31, 128, 256), BF),
            pltpu.VMEM((4, 128, 256), BF),
            pltpu.VMEM((4, 128, 256), BF),
            pltpu.VMEM((streams, 3, 4, 32, 256), BF),
            pltpu.VMEM((streams, 4, 32, 256), BF),
            pltpu.VMEM((streams, 3, 4, 16, 128), BF),
            pltpu.VMEM((groups, 8, 16, 128), BF),
            pltpu.VMEM((groups, 7, 16, 128), BF),
            pltpu.VMEM((864, 16, 128), BF),
            pltpu.SemaphoreType.DMA((SEMAPHORES,)),
        ],
        compiler_params=pltpu.CompilerParams(
            collective_id=0, has_side_effects=True, vmem_limit_bytes=36 * 1024 * 1024
        ),
        name="section_backward",
    )(*operands)
    hbm = pl.BlockSpec(memory_space=pltpu.HBM)
    return pl.pallas_call(
        deliver,
        out_shape=tuple(jax.ShapeDtypeStruct(x.shape, BF) for x in (fine_field, conv_weight, down_weight)),
        in_specs=[vmem] * 2,
        out_specs=(hbm, hbm, hbm),
        scratch_shapes=[pltpu.SemaphoreType.DMA((6,))],
        compiler_params=pltpu.CompilerParams(vmem_limit_bytes=1024 * 1024),
        name="deliver",
    )(*[pltpu.with_memory_space_constraint(r, pltpu.VMEM) for r in results])


def solution(mesh):
    in_specs = (P("gx", "gy", None, None), P(), P(), P("gx", "gy", None, None))
    out_specs = (P("gx", "gy", None, None), P(), P())
    return jax.shard_map(
        on_device, mesh=mesh, in_specs=in_specs, out_specs=out_specs, check_vma=False
    )
```

```python
import math

import jax
import jax.numpy as jnp
from jax import lax
from jax.experimental import pallas as pl
from jax.experimental.pallas import tpu as pltpu
from jax.sharding import PartitionSpec as P

MESH = pl.DeviceIdType.MESH
BF = jnp.bfloat16
F32 = jnp.float32

GROUPS = (
    ((0, 4, True), (4, 4, False)),
    ((8, 4, True), (12, 4, False)),
    ((16, 4, True), (20, 4, False)),
    ((24, 3, False), (27, 4, True)),
)
MOST = 4
RELAYED = (0, 1, 2)
RELAYED_SUMS = ()
CONV_TAPS = 27
SEMAPHORES = 57


def dot(a, b):
    return jnp.dot(a, b, preferred_element_type=F32)


def dot_t(a, b):
    return lax.dot_general(a, b, (((1,), (1,)), ((), ())), preferred_element_type=F32)


def iotas(n):
    return lax.broadcasted_iota(jnp.int32, (n, n), 0), lax.broadcasted_iota(jnp.int32, (n, n), 1)


def ones_where(mask):
    return jnp.where(mask, 1.0, 0.0).astype(BF)


def kernel(
    fine_in, down_in, conv_in, cot_in, fine_out, out,
    fine, down_w, conv_w, cot, x_mat, x_t, q, hs, ht, gp, gs, sums, part, part_in, r1, y0, y1, r2, z1, r3, measure, sems,
):
    gx, z = lax.axis_index("gx"), lax.axis_index("gy")
    px, py, c = gx // 8, (gx // 2) % 4, gx % 2

    def at(dx, dz):
        return ((gx + dx + 32) % 32, (z + dz + 8) % 8)

    def on_x(k):
        return ((((px + k) % 4) * 4 + py) * 2 + c, z)

    def on_y(k):
        return ((px * 4 + (py + k) % 4) * 2 + c, z)

    def on_z(k):
        return (gx, (z + k) % 8)

    partner = (gx + 1 - 2 * c, z)
    other = 2 * c - 1

    names, amounts = {}, {}

    def sem(name):
        return sems.at[names.setdefault(name, len(names))]

    def count(name, ref):
        amounts[name] = amounts.get(name, 0) + math.prod(ref.shape) // 2048

    def wait(name):
        tiles = measure.at[0 : amounts.pop(name)]
        pltpu.make_async_copy(tiles, tiles, sem(name)).wait()

    def wait_all():
        for name in list(amounts):
            wait(name)

    def load(src, dst, name):
        count(name, src)
        pltpu.make_async_copy(src, dst, sem(name)).start()

    def send(src, dst, sent, received, device):
        count(sent, src)
        count(received, src)
        pltpu.make_async_remote_copy(
            src_ref=src, dst_ref=dst, send_sem=sem(sent), recv_sem=sem(received), device_id=device, device_id_type=MESH
        ).start()

    load(fine_in, fine, "fine")
    load(down_in, down_w, "fine")
    load(cot_in, cot, "cot")
    load(conv_in, conv_w, "conv")

    greeted = [at(dx, dz) for dx in (-1, 0, 1) for dz in (-1, 0, 1) if (dx, dz) != (0, 0)]
    greeted += [on_x(k) for k in (1, 2, 3)] + [on_y(k) for k in (1, 2, 3)]
    greeted += [on_z(k) for k in range(2, 7)]
    barrier = pltpu.get_barrier_semaphore()
    for device in greeted:
        pl.semaphore_signal(barrier, inc=1, device_id=device, device_id_type=MESH)

    row, col = iotas(256)

    def target(r):
        group, j, k = r >> 6, (r >> 5) & 1, r & 31
        return (j * 2 + (group >> 1)) * 64 + 2 * k + (group & 1)

    sort = ones_where(col == target(row))
    before = ones_where((col == row - 1) & ((row & 31) != 0))
    after = ones_where((col == row + 1) & ((row & 31) != 31))
    r128, c128 = iotas(128)
    eye = ones_where(r128 == c128)
    wait("fine")
    for a in range(2):
        for block in range(4):
            rows = fine[a, 4 * block : 4 * block + 4].reshape(256, 128)
            sorted_rows = dot(sort, rows).astype(BF)
            for group in range(4):
                lane = (4 * a + group) * 128
                x_mat[64 * block : 64 * block + 64, lane : lane + 128] = sorted_rows[64 * group : 64 * group + 64]
    hidden = dot(x_mat[...], down_w[...].reshape(1024, 256)).astype(BF)
    mine = 1 + c
    for half in range(2):
        q[mine, half, 32:288, :] = hidden[:, 128 * half : 128 * half + 128]

    pl.semaphore_wait(barrier, len(greeted))

    whole, low, high = pl.ds(32, 256), pl.ds(256, 32), pl.ds(32, 32)
    first, last = pl.ds(0, 32), pl.ds(288, 32)
    sides = ((-other, 1 + c, 2 * c), (other, 3 * (1 - c), 2 - 2 * c), (0, 1 + c, 1))
    shifts = ((0, whole, whole), (1, low, first), (-1, high, last))

    def halo(kind, source_of, target_of):
        for dz, src, dst in shifts[1:] + shifts[:1]:
            for side in (2, 0, 1):
                if (dz, side) != (0, 2):
                    name = (kind, side, dz == 0 and kind == "grad")
                    send(source_of(src), target_of(side, dst), "halo sent", name, at(sides[side][0], dz))

    halo("hidden", lambda rows: q.at[mine, :, rows], lambda side, rows: q.at[sides[side][1], :, rows])
    for t in range(8):
        x_t[t] = dot_t(eye, x_mat[:, 128 * t : 128 * t + 128]).astype(BF)

    top, bottom = z > 0, z < 7
    other_ok = jnp.logical_and(gx + other >= 0, gx + other < 32)
    far_plane = 3 * c
    edges = ((slice(0, 32), top), (slice(288, 320), bottom))

    def clear(ref, index, rows, ok):
        old = ref[index + (rows,)]
        ref[index + (rows,)] = jnp.where(ok, old, jnp.zeros(old.shape, BF))

    acc = None
    for role, plane, a, side in ((0, mine, 1, 2), (1, 2 - c, 2 - 2 * c, 0), (2, far_plane, 2 * c, 1)):
        wait(("hidden", side, False))
        for rows, ok in edges:
            clear(q, (plane, slice(None)), rows, ok if side != 1 else jnp.logical_and(ok, other_ok))
        if side == 1:
            clear(q, (plane, slice(None)), slice(32, 288), other_ok)
            beyond = q.at[far_plane, 1 - c]
            send(beyond, beyond, "halo sent", "far", partner)
        elif side == 2:
            wait("conv")
        rows_of = jnp.concatenate([q[plane, 0], q[plane, 1]], axis=1)
        for i, shift in ((0, before), (1, after)):
            hs[i, role, 0:256] = dot(shift, rows_of[0:256]).astype(BF)
            hs[i, role, 256:320] = dot(shift[0:64, 0:64], rows_of[256:320]).astype(BF)
        pieces = []
        for b in range(3):
            rows = slice(32 * b, 32 * b + 256)
            pieces += [hs[0, role, rows], rows_of[rows], hs[1, role, rows]]
        taps = conv_w[pl.ds(9 * a, 9)].reshape(2304, 256)
        term = dot(jnp.concatenate(pieces, axis=1), taps)
        acc = term if acc is None else acc + term
    sig = jax.nn.sigmoid(acc)
    wait("cot")
    cotangent = cot[...].reshape(256, 256).astype(F32)
    gp[1, 32:288] = (cotangent * (sig * (1.0 + acc * (1.0 - sig)))).astype(BF)

    halo("grad", lambda rows: gp.at[1, rows], lambda side, rows: gp.at[sides[side][2], rows])
    wait("far")
    for plane in range(4):
        for b in range(3):
            ht[b, plane] = dot_t(eye, q[plane, c, 32 * b : 32 * b + 256]).astype(BF)
    for i, shift in ((0, after), (1, before)):
        gs[i, 1, 32:288] = dot(shift, gp[1, 32:288]).astype(BF)

    wait(("grad", 0, True))
    near = 2 - 2 * c
    for i, shift in ((0, after), (1, before)):
        gs[i, near, 32:288] = dot(shift, gp[near, 32:288]).astype(BF)

    halves = (slice(0, 16), slice(16, 32))

    def row_block(f):
        return pl.ds(pl.multiple_of(32 * f, 32), 32)

    class Stream:
        def __init__(self, group, half):
            self.i, self.group = 2 * group + half, group
            self.t0, self.n, x_first = GROUPS[group][half]
            self.tile0 = self.t0 - 8 * group
            self.f, self.s = (px, py) if x_first else (py, px)
            self.first, self.second = (on_x, on_y) if x_first else (on_y, on_x)
            self.row = c * 128 + 32 * self.f + 16 * (self.s % 2)
            self.lane = 128 * (self.s // 2)

        def send(self, src, dst, name, device):
            send(src, dst, ("sent", self.group), (name, self.group), device)

        def tile(self, s):
            return pl.ds(pl.multiple_of(16 * (s % 2), 16), 16), pl.ds(pl.multiple_of(128 * (s // 2), 128), 128)

        def half(self, f, h):
            return pl.ds(pl.multiple_of(32 * (f % 4) + 16 * h, 16), 16)

        def out_rows(self, f):
            rows = pl.ds(pl.multiple_of(c * 128 + 32 * f, 32), 32)
            return out.at[self.t0 : self.t0 + self.n, rows]

        def start_first(self):
            if self.group not in RELAYED_SUMS:
                for k in (1, 3, 2):
                    src = sums.at[self.t0 : self.t0 + self.n, row_block((self.f + k) % 4)]
                    self.send(src, r1.at[self.i, k - 1, 0 : self.n], "first", self.first(k))
                return
            for k in (1, 3):
                src = sums.at[self.t0 : self.t0 + self.n, self.half(self.f + 2, k // 2)]
                self.send(src, r1.at[self.i, 1, 0 : self.n, halves[k // 2]], "first relay", self.first(k))
            for k in (1, 3):
                src = sums.at[self.t0 : self.t0 + self.n, self.half(self.f + k, 1 - k // 2)]
                self.send(src, r1.at[self.i, k - 1, 0 : self.n, halves[1 - k // 2]], "first", self.first(k))

        def relay_first(self):
            for k in (1, 3):
                h = k // 2
                own = sums[self.t0 : self.t0 + self.n, self.half(self.f + k, h)].astype(F32)
                both = own + r1[self.i, 1, 0 : self.n, halves[h]].astype(F32)
                y0[self.i, h, 0 : self.n] = both.astype(BF)
                src = y0.at[self.i, h, 0 : self.n]
                self.send(src, r1.at[self.i, k - 1, 0 : self.n, halves[h]], "first", self.first(k))

        def start_second(self):
            total = sums[self.t0 : self.t0 + self.n, row_block(self.f)].astype(F32)
            for k in (0, 2) if self.group in RELAYED_SUMS else (0, 1, 2):
                total = total + r1[self.i, k, 0 : self.n].astype(F32)
            y1[self.i, 0 : self.n] = total.astype(BF)
            for k in (1, 3, 2):
                rows, lanes = self.tile((self.s + k) % 4)
                src = y1.at[self.i, 0 : self.n, rows, lanes]
                self.send(src, r2.at[self.i, k - 1, 0 : self.n], "second", self.second(k))

        def sum_second(self):
            rows, lanes = self.tile(self.s)
            total = y1[self.i, 0 : self.n, rows, lanes].astype(F32)
            for k in range(3):
                total = total + r2[self.i, k, 0 : self.n].astype(F32)
            z1[self.group, self.tile0 : self.tile0 + self.n] = total.astype(BF)

        def gather_second(self):
            rows = pl.ds(pl.multiple_of(self.row, 16), 16)
            lanes = pl.ds(pl.multiple_of(self.lane, 128), 128)
            here = out.at[self.t0 : self.t0 + self.n, rows, lanes]
            for k in (1, 3, 2):
                self.send(here, here, "gather second", self.second(k))

        def gather_first(self):
            here = self.out_rows(self.f)
            for k in (1, 3) if self.group in RELAYED else (1, 3, 2):
                self.send(here, here, ("gather first", k), self.first(k))
            self.send(here, here, "core", partner)

        def relay(self, k):
            f = (self.f + 4 - k) % 4
            if self.group in RELAYED:
                half = pl.ds(pl.multiple_of(c * 128 + 32 * f + 16 * (k // 2), 16), 16)
                here = out.at[self.t0 : self.t0 + self.n, half]
                self.send(here, here, ("gather first", 2), self.first(k))
            self.gather_core(k)

        def gather_core(self, k):
            here = self.out_rows((self.f + 4 - k) % 4)
            self.send(here, here, "core", partner)

    class Group:
        def __init__(self, index):
            self.i = index
            self.streams = [Stream(index, half) for half in range(2)]

        def send(self, src, dst, name, device):
            send(src, dst, ("sent", self.i), (name, self.i), device)

        def start_first(self):
            for stream in self.streams:
                stream.start_first()

        def relay_first(self):
            wait(("first relay", self.i))
            for stream in self.streams:
                stream.relay_first()

        def start_second(self):
            wait(("first", self.i))
            for stream in self.streams:
                stream.start_second()

        def start_third(self):
            wait(("second", self.i))
            for stream in self.streams:
                stream.sum_second()
            end = self.streams[1].tile0 + self.streams[1].n
            if end < 8:
                z1[self.i, end:8] = jnp.zeros((8 - end, 16, 128), BF)
            for k in (4, 3, 5, 2, 6, 1, 7):
                self.send(z1.at[self.i, (z + k) % 8], r3.at[self.i, k - 1], "third", on_z(k))

        def gather_third(self):
            wait(("third", self.i))
            total = z1[self.i, z].astype(F32)
            for k in range(7):
                total = total + r3[self.i, k].astype(F32)
            a, b = self.streams
            later = (z + 8 - b.tile0) // 8
            rows = pl.ds(pl.multiple_of(a.row + later * (b.row - a.row), 16), 16)
            lanes = pl.ds(pl.multiple_of(a.lane + later * (b.lane - a.lane), 128), 128)
            out[8 * self.i + z, rows, lanes] = total.astype(BF)
            here = out.at[8 * self.i + z, rows, lanes]
            for k in (4, 3, 5, 2, 6, 1, 7):
                self.send(here, here, "gather third", on_z(k))

        def gather_second(self):
            wait(("gather third", self.i))
            for stream in self.streams:
                stream.gather_second()

        def gather_first(self):
            wait(("gather second", self.i))
            for stream in self.streams:
                stream.gather_first()

        def relay(self):
            for k in (1, 3):
                wait((("gather first", k), self.i))
                for stream in self.streams:
                    stream.relay(k)

        def gather_core(self):
            wait((("gather first", 2), self.i))
            for stream in self.streams:
                stream.gather_core(2)

        def finish(self):
            wait(("core", self.i))

    groups = [Group(i) for i in range(len(GROUPS))]

    def grad_rows(s, p):
        a = p + 1 - c
        return gp[a, 32:288] if s == 1 else gs[s // 2, a, 32:288]

    both_planes = [jnp.concatenate([grad_rows(s, 0), grad_rows(s, 1)], axis=0) for s in range(3)]
    for t in range(CONV_TAPS):
        a, b, s = t // 9, (t // 3) % 3, t % 3
        lhs = jnp.concatenate([ht[b, a], ht[b, a + 1]], axis=1)
        sums[t] = dot(lhs, both_planes[s]).astype(BF)
        if t % 8 == 7:
            groups[t // 8].start_first()

    for name in (("grad", 2, False), ("grad", 0, False), ("grad", 1, False), ("grad", 1, True)):
        wait(name)
    away = 2 * c
    clear(gp, (away,), slice(32, 288), other_ok)
    for i, shift in ((0, after), (1, before)):
        gs[i, away, 32:288] = dot(shift, gp[away, 32:288]).astype(BF)
    for plane, valid in ((1, None), (near, None), (away, other_ok)):
        for rows, ok in edges:
            clear(gp, (plane,), rows, ok if valid is None else jnp.logical_and(ok, valid))
            for i, shift in ((0, after), (1, before)):
                gs[i, plane, rows] = dot(shift[0:32, 0:32], gp[plane, rows]).astype(BF)
    back = cotangent
    for a in range(3):
        for b in range(3):
            rows = slice(32 * (2 - b), 32 * (2 - b) + 256)
            for s in range(3):
                piece = gp[2 - a, rows] if s == 1 else gs[s // 2, 2 - a, rows]
                back = back + dot_t(piece, conv_w[9 * a + 3 * b + s])
    hidden_grad = back.astype(BF)
    for t in range(4):
        part[t] = dot(x_t[4 * (1 - c) + t], hidden_grad).astype(BF)
    send(part, part_in, "halo sent", "part", partner)

    unsort = ones_where(row == target(col))

    def write_fine(a):
        flat = [dot_t(hidden_grad, down_w[4 * a + g]).astype(BF) for g in range(4)]
        for block in range(4):
            rows = jnp.concatenate([f[64 * block : 64 * block + 64] for f in flat], axis=0)
            fine_out[a, 4 * block : 4 * block + 4] = dot(unsort, rows).astype(BF).reshape(4, 64, 128)

    groups[0].start_second()
    own = [dot(x_t[4 * c + t], hidden_grad) for t in range(4)]
    wait("part")
    for t in range(4):
        sums[27 + t] = (own[t] + part_in[t].astype(F32)).astype(BF)
    write_fine(0)
    groups[1].start_second()
    groups[3].start_first()
    write_fine(1)
    groups[0].start_third()
    groups[2].start_second()
    groups[1].start_third()
    groups[3].start_second()
    groups[2].start_third()
    groups[0].gather_third()
    groups[1].gather_third()
    groups[3].start_third()
    groups[2].gather_third()
    groups[0].gather_second()
    groups[1].gather_second()
    groups[3].gather_third()
    groups[0].gather_first()
    groups[2].gather_second()
    groups[1].gather_first()
    groups[3].gather_second()
    groups[0].relay()
    groups[2].gather_first()
    groups[1].relay()
    groups[3].gather_first()
    groups[0].gather_core()
    groups[2].relay()
    groups[1].gather_core()
    groups[3].relay()
    groups[2].gather_core()
    groups[3].gather_core()
    for group in groups:
        group.finish()
    wait_all()


def deliver(fine, sums, fine_out, conv_out, down_out, sems):
    moves = [(sums.at[t : t + 9], conv_out.at[t : t + 9]) for t in range(0, CONV_TAPS, 9)]
    moves.append((fine, fine_out))
    for core in range(2):
        taps = sums.at[CONV_TAPS : CONV_TAPS + 4, 128 * core : 128 * core + 128]
        moves.append((taps, down_out.at[4 * core : 4 * core + 4]))
    copies = []
    for i, (src, dst) in enumerate(moves):
        copy = pltpu.make_async_copy(src, dst, sems.at[i])
        copy.start()
        copies.append(copy)
    for copy in copies:
        copy.wait()


def on_device(fine_field, down_weight, conv_weight, coarse_cotangent):
    vmem = pl.BlockSpec(memory_space=pltpu.VMEM)
    groups, streams = len(GROUPS), 2 * len(GROUPS)
    operands = (fine_field, down_weight, conv_weight, coarse_cotangent)
    operands = [pltpu.with_memory_space_constraint(x, pltpu.HBM) for x in operands]
    results = pl.pallas_call(
        kernel,
        out_shape=(
            jax.ShapeDtypeStruct(fine_field.shape, BF),
            jax.ShapeDtypeStruct((32, 256, 256), BF),
        ),
        in_specs=[pl.BlockSpec(memory_space=pltpu.HBM)] * 4,
        out_specs=(vmem, vmem),
        scratch_shapes=[
            pltpu.VMEM(fine_field.shape, BF),
            pltpu.VMEM(down_weight.shape, BF),
            pltpu.VMEM(conv_weight.shape, BF),
            pltpu.VMEM(coarse_cotangent.shape, BF),
            pltpu.VMEM((256, 1024), BF),
            pltpu.VMEM((8, 128, 256), BF),
            pltpu.VMEM((4, 2, 320, 128), BF),
            pltpu.VMEM((2, 3, 320, 256), BF),
            pltpu.VMEM((3, 4, 128, 256), BF),
            pltpu.VMEM((3, 320, 256), BF),
            pltpu.VMEM((2, 3, 320, 256), BF),
            pltpu.VMEM((31, 128, 256), BF),
            pltpu.VMEM((4, 128, 256), BF),
            pltpu.VMEM((4, 128, 256), BF),
            pltpu.VMEM((streams, 3, MOST, 32, 256), BF),
            pltpu.VMEM((streams, 2, MOST, 16, 256), BF),
            pltpu.VMEM((streams, MOST, 32, 256), BF),
            pltpu.VMEM((streams, 3, MOST, 16, 128), BF),
            pltpu.VMEM((groups, 8, 16, 128), BF),
            pltpu.VMEM((groups, 7, 16, 128), BF),
            pltpu.VMEM((864, 16, 128), BF),
            pltpu.SemaphoreType.DMA((SEMAPHORES,)),
        ],
        compiler_params=pltpu.CompilerParams(
            collective_id=0, has_side_effects=True, vmem_limit_bytes=36 * 1024 * 1024
        ),
        name="section_backward",
    )(*operands)
    hbm = pl.BlockSpec(memory_space=pltpu.HBM)
    return pl.pallas_call(
        deliver,
        out_shape=tuple(jax.ShapeDtypeStruct(x.shape, BF) for x in (fine_field, conv_weight, down_weight)),
        in_specs=[vmem] * 2,
        out_specs=(hbm, hbm, hbm),
        scratch_shapes=[pltpu.SemaphoreType.DMA((6,))],
        compiler_params=pltpu.CompilerParams(vmem_limit_bytes=1024 * 1024),
        name="deliver",
    )(*[pltpu.with_memory_space_constraint(r, pltpu.VMEM) for r in results])


def solution(mesh):
    in_specs = (P("gx", "gy", None, None), P(), P(), P("gx", "gy", None, None))
    out_specs = (P("gx", "gy", None, None), P(), P())
    return jax.shard_map(
        on_device, mesh=mesh, in_specs=in_specs, out_specs=out_specs, check_vma=False
    )
```

```python
import math

import jax
import jax.numpy as jnp
from jax import lax
from jax.experimental import pallas as pl
from jax.experimental.pallas import tpu as pltpu
from jax.sharding import PartitionSpec as P

MESH = pl.DeviceIdType.MESH
BF = jnp.bfloat16
F32 = jnp.float32

GROUPS = (
    ((0, 4, True), (4, 4, False)),
    ((8, 4, True), (12, 4, False)),
    ((16, 4, True), (20, 4, False)),
    ((24, 3, False), (27, 4, True)),
)
MOST = 4
RELAYED = (0, 1, 2)
CONV_TAPS = 27
SEMAPHORES = 54


def dot(a, b):
    return jnp.dot(a, b, preferred_element_type=F32)


def dot_t(a, b):
    return lax.dot_general(a, b, (((1,), (1,)), ((), ())), preferred_element_type=F32)


def iotas(n):
    return lax.broadcasted_iota(jnp.int32, (n, n), 0), lax.broadcasted_iota(jnp.int32, (n, n), 1)


def ones_where(mask):
    return jnp.where(mask, 1.0, 0.0).astype(BF)


def kernel(
    fine_in, down_in, conv_in, cot_in, fine_out, out,
    fine, down_w, conv_w, cot, x_mat, x_t, q, hs, ht, gp, gs, sums, part, part_in, r1, y1, r2, z1, r3, measure, sems,
):
    gx, z = lax.axis_index("gx"), lax.axis_index("gy")
    px, py, c = gx // 8, (gx // 2) % 4, gx % 2

    def at(dx, dz):
        return ((gx + dx + 32) % 32, (z + dz + 8) % 8)

    def on_x(k):
        return ((((px + k) % 4) * 4 + py) * 2 + c, z)

    def on_y(k):
        return ((px * 4 + (py + k) % 4) * 2 + c, z)

    def on_z(k):
        return (gx, (z + k) % 8)

    partner = (gx + 1 - 2 * c, z)
    other = 2 * c - 1

    names, amounts = {}, {}

    def sem(name):
        return sems.at[names.setdefault(name, len(names))]

    def count(name, ref):
        amounts[name] = amounts.get(name, 0) + math.prod(ref.shape) // 2048

    def wait(name):
        tiles = measure.at[0 : amounts.pop(name)]
        pltpu.make_async_copy(tiles, tiles, sem(name)).wait()

    def wait_all():
        for name in list(amounts):
            wait(name)

    def load(src, dst, name):
        count(name, src)
        pltpu.make_async_copy(src, dst, sem(name)).start()

    def send(src, dst, sent, received, device):
        count(sent, src)
        count(received, src)
        pltpu.make_async_remote_copy(
            src_ref=src, dst_ref=dst, send_sem=sem(sent), recv_sem=sem(received), device_id=device, device_id_type=MESH
        ).start()

    load(fine_in, fine, "fine")
    load(down_in, down_w, "fine")
    load(cot_in, cot, "cot")
    load(conv_in, conv_w, "conv")

    greeted = [at(dx, dz) for dx in (-1, 0, 1) for dz in (-1, 0, 1) if (dx, dz) != (0, 0)]
    greeted += [on_x(k) for k in (1, 2, 3)] + [on_y(k) for k in (1, 2, 3)]
    greeted += [on_z(k) for k in range(2, 7)]
    barrier = pltpu.get_barrier_semaphore()
    for device in greeted:
        pl.semaphore_signal(barrier, inc=1, device_id=device, device_id_type=MESH)

    row, col = iotas(256)

    def target(r):
        group, j, k = r >> 6, (r >> 5) & 1, r & 31
        return (j * 2 + (group >> 1)) * 64 + 2 * k + (group & 1)

    sort = ones_where(col == target(row))
    before = ones_where((col == row - 1) & ((row & 31) != 0))
    after = ones_where((col == row + 1) & ((row & 31) != 31))
    r128, c128 = iotas(128)
    eye = ones_where(r128 == c128)
    wait("fine")
    for a in range(2):
        for block in range(4):
            rows = fine[a, 4 * block : 4 * block + 4].reshape(256, 128)
            sorted_rows = dot(sort, rows).astype(BF)
            for group in range(4):
                lane = (4 * a + group) * 128
                x_mat[64 * block : 64 * block + 64, lane : lane + 128] = sorted_rows[64 * group : 64 * group + 64]
    hidden = dot(x_mat[...], down_w[...].reshape(1024, 256)).astype(BF)
    mine = 1 + c
    for half in range(2):
        q[mine, half, 32:288, :] = hidden[:, 128 * half : 128 * half + 128]

    pl.semaphore_wait(barrier, len(greeted))

    whole, low, high = pl.ds(32, 256), pl.ds(256, 32), pl.ds(32, 32)
    first, last = pl.ds(0, 32), pl.ds(288, 32)
    sides = ((-other, 1 + c, 2 * c), (other, 3 * (1 - c), 2 - 2 * c), (0, 1 + c, 1))
    shifts = ((0, whole, whole), (1, low, first), (-1, high, last))

    def halo(kind, source_of, target_of):
        for dz, src, dst in shifts[1:] + shifts[:1]:
            for side in (2, 0, 1):
                if (dz, side) != (0, 2):
                    name = (kind, side, dz == 0 and kind == "grad")
                    send(source_of(src), target_of(side, dst), "halo sent", name, at(sides[side][0], dz))

    halo("hidden", lambda rows: q.at[mine, :, rows], lambda side, rows: q.at[sides[side][1], :, rows])
    for t in range(8):
        x_t[t] = dot_t(eye, x_mat[:, 128 * t : 128 * t + 128]).astype(BF)

    top, bottom = z > 0, z < 7
    other_ok = jnp.logical_and(gx + other >= 0, gx + other < 32)
    far_plane = 3 * c
    edges = ((slice(0, 32), top), (slice(288, 320), bottom))

    def clear(ref, index, rows, ok):
        old = ref[index + (rows,)]
        ref[index + (rows,)] = jnp.where(ok, old, jnp.zeros(old.shape, BF))

    def transpose(plane):
        for b in range(3):
            ht[b, plane] = dot_t(eye, q[plane, c, 32 * b : 32 * b + 256]).astype(BF)

    acc = None
    for role, plane, a, side in ((0, mine, 1, 2), (1, 2 - c, 2 - 2 * c, 0), (2, far_plane, 2 * c, 1)):
        wait(("hidden", side, False))
        for rows, ok in edges:
            clear(q, (plane, slice(None)), rows, ok if side != 1 else jnp.logical_and(ok, other_ok))
        if side == 1:
            clear(q, (plane, slice(None)), slice(32, 288), other_ok)
            beyond = q.at[far_plane, 1 - c]
            send(beyond, beyond, "halo sent", "far", partner)
        elif side == 2:
            wait("conv")
        rows_of = jnp.concatenate([q[plane, 0], q[plane, 1]], axis=1)
        for i, shift in ((0, before), (1, after)):
            hs[i, role, 0:256] = dot(shift, rows_of[0:256]).astype(BF)
            hs[i, role, 256:320] = dot(shift[0:64, 0:64], rows_of[256:320]).astype(BF)
        pieces = []
        for b in range(3):
            rows = slice(32 * b, 32 * b + 256)
            pieces += [hs[0, role, rows], rows_of[rows], hs[1, role, rows]]
        taps = conv_w[pl.ds(9 * a, 9)].reshape(2304, 256)
        term = dot(jnp.concatenate(pieces, axis=1), taps)
        acc = term if acc is None else acc + term
        if side != 1:
            transpose(plane)
    sig = jax.nn.sigmoid(acc)
    wait("cot")
    cotangent = cot[...].reshape(256, 256).astype(F32)
    gp[1, 32:288] = (cotangent * (sig * (1.0 + acc * (1.0 - sig)))).astype(BF)

    halo("grad", lambda rows: gp.at[1, rows], lambda side, rows: gp.at[sides[side][2], rows])
    transpose(far_plane)
    wait("far")
    transpose(3 - far_plane)
    for i, shift in ((0, after), (1, before)):
        gs[i, 1, 32:288] = dot(shift, gp[1, 32:288]).astype(BF)

    wait(("grad", 0, True))
    near = 2 - 2 * c
    for i, shift in ((0, after), (1, before)):
        gs[i, near, 32:288] = dot(shift, gp[near, 32:288]).astype(BF)

    def row_block(f):
        return pl.ds(pl.multiple_of(32 * f, 32), 32)

    class Stream:
        def __init__(self, group, half):
            self.i, self.group = 2 * group + half, group
            self.t0, self.n, x_first = GROUPS[group][half]
            self.tile0 = self.t0 - 8 * group
            self.f, self.s = (px, py) if x_first else (py, px)
            self.first, self.second = (on_x, on_y) if x_first else (on_y, on_x)
            self.row = c * 128 + 32 * self.f + 16 * (self.s % 2)
            self.lane = 128 * (self.s // 2)

        def send(self, src, dst, name, device):
            send(src, dst, ("sent", self.group), (name, self.group), device)

        def tile(self, s):
            return pl.ds(pl.multiple_of(16 * (s % 2), 16), 16), pl.ds(pl.multiple_of(128 * (s // 2), 128), 128)

        def out_rows(self, f):
            rows = pl.ds(pl.multiple_of(c * 128 + 32 * f, 32), 32)
            return out.at[self.t0 : self.t0 + self.n, rows]

        def start_first(self):
            for k in (1, 3, 2):
                src = sums.at[self.t0 : self.t0 + self.n, row_block((self.f + k) % 4)]
                self.send(src, r1.at[self.i, k - 1, 0 : self.n], "first", self.first(k))

        def start_second(self):
            total = sums[self.t0 : self.t0 + self.n, row_block(self.f)].astype(F32)
            for k in range(3):
                total = total + r1[self.i, k, 0 : self.n].astype(F32)
            y1[self.i, 0 : self.n] = total.astype(BF)
            for k in (1, 3, 2):
                rows, lanes = self.tile((self.s + k) % 4)
                src = y1.at[self.i, 0 : self.n, rows, lanes]
                self.send(src, r2.at[self.i, k - 1, 0 : self.n], "second", self.second(k))

        def sum_second(self):
            rows, lanes = self.tile(self.s)
            total = y1[self.i, 0 : self.n, rows, lanes].astype(F32)
            for k in range(3):
                total = total + r2[self.i, k, 0 : self.n].astype(F32)
            z1[self.group, self.tile0 : self.tile0 + self.n] = total.astype(BF)

        def gather_second(self):
            rows = pl.ds(pl.multiple_of(self.row, 16), 16)
            lanes = pl.ds(pl.multiple_of(self.lane, 128), 128)
            here = out.at[self.t0 : self.t0 + self.n, rows, lanes]
            for k in (1, 3, 2):
                self.send(here, here, "gather second", self.second(k))

        def gather_first(self):
            here = self.out_rows(self.f)
            for k in (1, 3) if self.group in RELAYED else (1, 3, 2):
                self.send(here, here, ("gather first", k), self.first(k))
            self.send(here, here, "core", partner)

        def relay(self, k):
            f = (self.f + 4 - k) % 4
            if self.group in RELAYED:
                half = pl.ds(pl.multiple_of(c * 128 + 32 * f + 16 * (k // 2), 16), 16)
                here = out.at[self.t0 : self.t0 + self.n, half]
                self.send(here, here, ("gather first", 2), self.first(k))
            self.gather_core(k)

        def gather_core(self, k):
            here = self.out_rows((self.f + 4 - k) % 4)
            self.send(here, here, "core", partner)

    class Group:
        def __init__(self, index):
            self.i = index
            self.streams = [Stream(index, half) for half in range(2)]

        def send(self, src, dst, name, device):
            send(src, dst, ("sent", self.i), (name, self.i), device)

        def start_first(self):
            for stream in self.streams:
                stream.start_first()

        def start_second(self):
            wait(("first", self.i))
            for stream in self.streams:
                stream.start_second()

        def start_third(self):
            wait(("second", self.i))
            for stream in self.streams:
                stream.sum_second()
            end = self.streams[1].tile0 + self.streams[1].n
            if end < 8:
                z1[self.i, end:8] = jnp.zeros((8 - end, 16, 128), BF)
            for k in (4, 3, 5, 2, 6, 1, 7):
                self.send(z1.at[self.i, (z + k) % 8], r3.at[self.i, k - 1], "third", on_z(k))

        def gather_third(self):
            wait(("third", self.i))
            total = z1[self.i, z].astype(F32)
            for k in range(7):
                total = total + r3[self.i, k].astype(F32)
            a, b = self.streams
            later = (z + 8 - b.tile0) // 8
            rows = pl.ds(pl.multiple_of(a.row + later * (b.row - a.row), 16), 16)
            lanes = pl.ds(pl.multiple_of(a.lane + later * (b.lane - a.lane), 128), 128)
            out[8 * self.i + z, rows, lanes] = total.astype(BF)
            here = out.at[8 * self.i + z, rows, lanes]
            for k in (4, 3, 5, 2, 6, 1, 7):
                self.send(here, here, "gather third", on_z(k))

        def gather_second(self):
            wait(("gather third", self.i))
            for stream in self.streams:
                stream.gather_second()

        def gather_first(self):
            wait(("gather second", self.i))
            for stream in self.streams:
                stream.gather_first()

        def relay(self):
            for k in (1, 3):
                wait((("gather first", k), self.i))
                for stream in self.streams:
                    stream.relay(k)

        def gather_core(self):
            wait((("gather first", 2), self.i))
            for stream in self.streams:
                stream.gather_core(2)

        def finish(self):
            wait(("core", self.i))

    groups = [Group(i) for i in range(len(GROUPS))]

    def grad_rows(s, p):
        a = p + 1 - c
        return gp[a, 32:288] if s == 1 else gs[s // 2, a, 32:288]

    both_planes = [jnp.concatenate([grad_rows(s, 0), grad_rows(s, 1)], axis=0) for s in range(3)]
    for t in range(CONV_TAPS):
        a, b, s = t // 9, (t // 3) % 3, t % 3
        lhs = jnp.concatenate([ht[b, a], ht[b, a + 1]], axis=1)
        sums[t] = dot(lhs, both_planes[s]).astype(BF)
        if t % 8 == 7:
            groups[t // 8].start_first()

    for name in (("grad", 2, False), ("grad", 0, False), ("grad", 1, False), ("grad", 1, True)):
        wait(name)
    away = 2 * c
    clear(gp, (away,), slice(32, 288), other_ok)
    for i, shift in ((0, after), (1, before)):
        gs[i, away, 32:288] = dot(shift, gp[away, 32:288]).astype(BF)
    for plane, valid in ((1, None), (near, None), (away, other_ok)):
        for rows, ok in edges:
            clear(gp, (plane,), rows, ok if valid is None else jnp.logical_and(ok, valid))
            for i, shift in ((0, after), (1, before)):
                gs[i, plane, rows] = dot(shift[0:32, 0:32], gp[plane, rows]).astype(BF)
    back = cotangent
    for a in range(3):
        for b in range(3):
            rows = slice(32 * (2 - b), 32 * (2 - b) + 256)
            for s in range(3):
                piece = gp[2 - a, rows] if s == 1 else gs[s // 2, 2 - a, rows]
                back = back + dot_t(piece, conv_w[9 * a + 3 * b + s])
    hidden_grad = back.astype(BF)
    for t in range(4):
        part[t] = dot(x_t[4 * (1 - c) + t], hidden_grad).astype(BF)
    send(part, part_in, "halo sent", "part", partner)

    unsort = ones_where(row == target(col))

    def write_fine(a):
        flat = [dot_t(hidden_grad, down_w[4 * a + g]).astype(BF) for g in range(4)]
        for block in range(4):
            rows = jnp.concatenate([f[64 * block : 64 * block + 64] for f in flat], axis=0)
            fine_out[a, 4 * block : 4 * block + 4] = dot(unsort, rows).astype(BF).reshape(4, 64, 128)

    groups[0].start_second()
    own = [dot(x_t[4 * c + t], hidden_grad) for t in range(4)]
    wait("part")
    for t in range(4):
        sums[27 + t] = (own[t] + part_in[t].astype(F32)).astype(BF)
    groups[1].start_second()
    groups[3].start_first()
    groups[0].start_third()
    groups[2].start_second()
    groups[1].start_third()
    write_fine(0)
    write_fine(1)
    groups[3].start_second()
    groups[2].start_third()
    groups[0].gather_third()
    groups[1].gather_third()
    groups[3].start_third()
    groups[2].gather_third()
    groups[0].gather_second()
    groups[1].gather_second()
    groups[3].gather_third()
    groups[0].gather_first()
    groups[2].gather_second()
    groups[1].gather_first()
    groups[3].gather_second()
    groups[0].relay()
    groups[2].gather_first()
    groups[1].relay()
    groups[3].gather_first()
    groups[0].gather_core()
    groups[2].relay()
    groups[1].gather_core()
    groups[3].relay()
    groups[2].gather_core()
    groups[3].gather_core()
    for group in groups:
        group.finish()
    wait_all()


def deliver(fine, sums, fine_out, conv_out, down_out, sems):
    moves = [(sums.at[t : t + 9], conv_out.at[t : t + 9]) for t in range(0, CONV_TAPS, 9)]
    moves.append((fine, fine_out))
    for core in range(2):
        taps = sums.at[CONV_TAPS : CONV_TAPS + 4, 128 * core : 128 * core + 128]
        moves.append((taps, down_out.at[4 * core : 4 * core + 4]))
    copies = []
    for i, (src, dst) in enumerate(moves):
        copy = pltpu.make_async_copy(src, dst, sems.at[i])
        copy.start()
        copies.append(copy)
    for copy in copies:
        copy.wait()


def on_device(fine_field, down_weight, conv_weight, coarse_cotangent):
    vmem = pl.BlockSpec(memory_space=pltpu.VMEM)
    groups, streams = len(GROUPS), 2 * len(GROUPS)
    operands = (fine_field, down_weight, conv_weight, coarse_cotangent)
    operands = [pltpu.with_memory_space_constraint(x, pltpu.HBM) for x in operands]
    results = pl.pallas_call(
        kernel,
        out_shape=(
            jax.ShapeDtypeStruct(fine_field.shape, BF),
            jax.ShapeDtypeStruct((32, 256, 256), BF),
        ),
        in_specs=[pl.BlockSpec(memory_space=pltpu.HBM)] * 4,
        out_specs=(vmem, vmem),
        scratch_shapes=[
            pltpu.VMEM(fine_field.shape, BF),
            pltpu.VMEM(down_weight.shape, BF),
            pltpu.VMEM(conv_weight.shape, BF),
            pltpu.VMEM(coarse_cotangent.shape, BF),
            pltpu.VMEM((256, 1024), BF),
            pltpu.VMEM((8, 128, 256), BF),
            pltpu.VMEM((4, 2, 320, 128), BF),
            pltpu.VMEM((2, 3, 320, 256), BF),
            pltpu.VMEM((3, 4, 128, 256), BF),
            pltpu.VMEM((3, 320, 256), BF),
            pltpu.VMEM((2, 3, 320, 256), BF),
            pltpu.VMEM((31, 128, 256), BF),
            pltpu.VMEM((4, 128, 256), BF),
            pltpu.VMEM((4, 128, 256), BF),
            pltpu.VMEM((streams, 3, MOST, 32, 256), BF),
            pltpu.VMEM((streams, MOST, 32, 256), BF),
            pltpu.VMEM((streams, 3, MOST, 16, 128), BF),
            pltpu.VMEM((groups, 8, 16, 128), BF),
            pltpu.VMEM((groups, 7, 16, 128), BF),
            pltpu.VMEM((864, 16, 128), BF),
            pltpu.SemaphoreType.DMA((SEMAPHORES,)),
        ],
        compiler_params=pltpu.CompilerParams(
            collective_id=0, has_side_effects=True, vmem_limit_bytes=36 * 1024 * 1024
        ),
        name="section_backward",
    )(*operands)
    hbm = pl.BlockSpec(memory_space=pltpu.HBM)
    return pl.pallas_call(
        deliver,
        out_shape=tuple(jax.ShapeDtypeStruct(x.shape, BF) for x in (fine_field, conv_weight, down_weight)),
        in_specs=[vmem] * 2,
        out_specs=(hbm, hbm, hbm),
        scratch_shapes=[pltpu.SemaphoreType.DMA((6,))],
        compiler_params=pltpu.CompilerParams(vmem_limit_bytes=1024 * 1024),
        name="deliver",
    )(*[pltpu.with_memory_space_constraint(r, pltpu.VMEM) for r in results])


def solution(mesh):
    in_specs = (P("gx", "gy", None, None), P(), P(), P("gx", "gy", None, None))
    out_specs = (P("gx", "gy", None, None), P(), P())
    return jax.shard_map(
        on_device, mesh=mesh, in_specs=in_specs, out_specs=out_specs, check_vma=False
    )
```

```python
import math

import jax
import jax.numpy as jnp
from jax import lax
from jax.experimental import pallas as pl
from jax.experimental.pallas import tpu as pltpu
from jax.sharding import PartitionSpec as P

MESH = pl.DeviceIdType.MESH
BF = jnp.bfloat16
F32 = jnp.float32

GROUPS = (
    ((0, 4, True), (4, 4, False)),
    ((8, 4, True), (12, 4, False)),
    ((16, 4, True), (20, 4, False)),
    ((24, 3, False), (27, 4, True)),
)
MOST = 4
RELAYED = (0, 1, 2)
CONV_TAPS = 27
SEMAPHORES = 54


def dot(a, b):
    return jnp.dot(a, b, preferred_element_type=F32)


def dot_t(a, b):
    return lax.dot_general(a, b, (((1,), (1,)), ((), ())), preferred_element_type=F32)


def iotas(n):
    return lax.broadcasted_iota(jnp.int32, (n, n), 0), lax.broadcasted_iota(jnp.int32, (n, n), 1)


def ones_where(mask):
    return jnp.where(mask, 1.0, 0.0).astype(BF)


def kernel(
    fine_in, down_in, conv_in, cot_in, fine_out, out,
    fine, down_w, conv_w, cot, x_mat, x_t, q, hs, ht, gp, gs, sums, part, part_in, r1, y1, r2, z1, r3, measure, sems,
):
    gx, z = lax.axis_index("gx"), lax.axis_index("gy")
    px, py, c = gx // 8, (gx // 2) % 4, gx % 2

    def at(dx, dz):
        return ((gx + dx + 32) % 32, (z + dz + 8) % 8)

    def on_x(k):
        return ((((px + k) % 4) * 4 + py) * 2 + c, z)

    def on_y(k):
        return ((px * 4 + (py + k) % 4) * 2 + c, z)

    def on_z(k):
        return (gx, (z + k) % 8)

    partner = (gx + 1 - 2 * c, z)
    other = 2 * c - 1

    names, amounts = {}, {}

    def sem(name):
        return sems.at[names.setdefault(name, len(names))]

    def count(name, ref):
        amounts[name] = amounts.get(name, 0) + math.prod(ref.shape) // 2048

    def wait(name):
        tiles = measure.at[0 : amounts.pop(name)]
        pltpu.make_async_copy(tiles, tiles, sem(name)).wait()

    def wait_all():
        for name in list(amounts):
            wait(name)

    def load(src, dst, name):
        count(name, src)
        pltpu.make_async_copy(src, dst, sem(name)).start()

    def send(src, dst, sent, received, device):
        count(sent, src)
        count(received, src)
        pltpu.make_async_remote_copy(
            src_ref=src, dst_ref=dst, send_sem=sem(sent), recv_sem=sem(received), device_id=device, device_id_type=MESH
        ).start()

    load(fine_in, fine, "fine")
    load(down_in, down_w, "fine")
    load(cot_in, cot, "cot")
    load(conv_in, conv_w, "conv")

    greeted = [at(dx, dz) for dx in (-1, 0, 1) for dz in (-1, 0, 1) if (dx, dz) != (0, 0)]
    greeted += [on_x(k) for k in (1, 2, 3)] + [on_y(k) for k in (1, 2, 3)]
    greeted += [on_z(k) for k in range(2, 7)]
    barrier = pltpu.get_barrier_semaphore()
    for device in greeted:
        pl.semaphore_signal(barrier, inc=1, device_id=device, device_id_type=MESH)

    row, col = iotas(256)

    def target(r):
        group, j, k = r >> 6, (r >> 5) & 1, r & 31
        return (j * 2 + (group >> 1)) * 64 + 2 * k + (group & 1)

    sort = ones_where(col == target(row))
    before = ones_where((col == row - 1) & ((row & 31) != 0))
    after = ones_where((col == row + 1) & ((row & 31) != 31))
    r128, c128 = iotas(128)
    eye = ones_where(r128 == c128)
    wait("fine")
    for a in range(2):
        for block in range(4):
            rows = fine[a, 4 * block : 4 * block + 4].reshape(256, 128)
            sorted_rows = dot(sort, rows).astype(BF)
            for group in range(4):
                lane = (4 * a + group) * 128
                x_mat[64 * block : 64 * block + 64, lane : lane + 128] = sorted_rows[64 * group : 64 * group + 64]
    hidden = dot(x_mat[...], down_w[...].reshape(1024, 256)).astype(BF)
    mine = 1 + c
    for half in range(2):
        q[mine, half, 32:288, :] = hidden[:, 128 * half : 128 * half + 128]

    pl.semaphore_wait(barrier, len(greeted))

    whole, low, high = pl.ds(32, 256), pl.ds(256, 32), pl.ds(32, 32)
    first, last = pl.ds(0, 32), pl.ds(288, 32)
    sides = ((-other, 1 + c, 2 * c), (other, 3 * (1 - c), 2 - 2 * c), (0, 1 + c, 1))
    shifts = ((0, whole, whole), (1, low, first), (-1, high, last))

    def halo(kind, source_of, target_of):
        for dz, src, dst in shifts[1:] + shifts[:1]:
            for side in (2, 0, 1):
                if (dz, side) != (0, 2):
                    name = (kind, side, dz == 0 and kind == "grad")
                    send(source_of(src), target_of(side, dst), "halo sent", name, at(sides[side][0], dz))

    halo("hidden", lambda rows: q.at[mine, :, rows], lambda side, rows: q.at[sides[side][1], :, rows])
    for t in range(8):
        x_t[t] = dot_t(eye, x_mat[:, 128 * t : 128 * t + 128]).astype(BF)

    top, bottom = z > 0, z < 7
    other_ok = jnp.logical_and(gx + other >= 0, gx + other < 32)
    far_plane = 3 * c
    edges = ((slice(0, 32), top), (slice(288, 320), bottom))

    def clear(ref, index, rows, ok):
        old = ref[index + (rows,)]
        ref[index + (rows,)] = jnp.where(ok, old, jnp.zeros(old.shape, BF))

    def transpose(plane):
        for b in range(3):
            ht[b, plane] = dot_t(eye, q[plane, c, 32 * b : 32 * b + 256]).astype(BF)

    acc = None
    for role, plane, a, side in ((0, mine, 1, 2), (1, 2 - c, 2 - 2 * c, 0), (2, far_plane, 2 * c, 1)):
        wait(("hidden", side, False))
        for rows, ok in edges:
            clear(q, (plane, slice(None)), rows, ok if side != 1 else jnp.logical_and(ok, other_ok))
        if side == 1:
            clear(q, (plane, slice(None)), slice(32, 288), other_ok)
            beyond = q.at[far_plane, 1 - c]
            send(beyond, beyond, "halo sent", "far", partner)
        elif side == 2:
            wait("conv")
        rows_of = jnp.concatenate([q[plane, 0], q[plane, 1]], axis=1)
        for i, shift in ((0, before), (1, after)):
            hs[i, role, 0:256] = dot(shift, rows_of[0:256]).astype(BF)
            hs[i, role, 256:320] = dot(shift[0:64, 0:64], rows_of[256:320]).astype(BF)
        pieces = []
        for b in range(3):
            rows = slice(32 * b, 32 * b + 256)
            pieces += [hs[0, role, rows], rows_of[rows], hs[1, role, rows]]
        taps = conv_w[pl.ds(9 * a, 9)].reshape(2304, 256)
        term = dot(jnp.concatenate(pieces, axis=1), taps)
        acc = term if acc is None else acc + term
        if side != 1:
            transpose(plane)
    sig = jax.nn.sigmoid(acc)
    wait("cot")
    cotangent = cot[...].reshape(256, 256).astype(F32)
    gp[1, 32:288] = (cotangent * (sig * (1.0 + acc * (1.0 - sig)))).astype(BF)

    halo("grad", lambda rows: gp.at[1, rows], lambda side, rows: gp.at[sides[side][2], rows])
    transpose(far_plane)
    wait("far")
    transpose(3 - far_plane)
    for i, shift in ((0, after), (1, before)):
        gs[i, 1, 32:288] = dot(shift, gp[1, 32:288]).astype(BF)

    wait(("grad", 0, True))
    near = 2 - 2 * c
    for i, shift in ((0, after), (1, before)):
        gs[i, near, 32:288] = dot(shift, gp[near, 32:288]).astype(BF)

    def row_block(f):
        return pl.ds(pl.multiple_of(32 * f, 32), 32)

    class Stream:
        def __init__(self, group, half):
            self.i, self.group = 2 * group + half, group
            self.t0, self.n, x_first = GROUPS[group][half]
            self.tile0 = self.t0 - 8 * group
            self.f, self.s = (px, py) if x_first else (py, px)
            self.first, self.second = (on_x, on_y) if x_first else (on_y, on_x)
            self.row = c * 128 + 32 * self.f + 16 * (self.s % 2)
            self.lane = 128 * (self.s // 2)

        def send(self, src, dst, name, device):
            send(src, dst, ("sent", self.group), (name, self.group), device)

        def tile(self, s):
            return pl.ds(pl.multiple_of(16 * (s % 2), 16), 16), pl.ds(pl.multiple_of(128 * (s // 2), 128), 128)

        def out_rows(self, f):
            rows = pl.ds(pl.multiple_of(c * 128 + 32 * f, 32), 32)
            return out.at[self.t0 : self.t0 + self.n, rows]

        def start_first(self):
            for k in (1, 3, 2):
                src = sums.at[self.t0 : self.t0 + self.n, row_block((self.f + k) % 4)]
                self.send(src, r1.at[self.i, k - 1, 0 : self.n], "first", self.first(k))

        def start_second(self):
            total = sums[self.t0 : self.t0 + self.n, row_block(self.f)].astype(F32)
            for k in range(3):
                total = total + r1[self.i, k, 0 : self.n].astype(F32)
            y1[self.i, 0 : self.n] = total.astype(BF)
            for k in (1, 3, 2):
                rows, lanes = self.tile((self.s + k) % 4)
                src = y1.at[self.i, 0 : self.n, rows, lanes]
                self.send(src, r2.at[self.i, k - 1, 0 : self.n], "second", self.second(k))

        def sum_second(self):
            rows, lanes = self.tile(self.s)
            total = y1[self.i, 0 : self.n, rows, lanes].astype(F32)
            for k in range(3):
                total = total + r2[self.i, k, 0 : self.n].astype(F32)
            z1[self.group, self.tile0 : self.tile0 + self.n] = total.astype(BF)

        def gather_second(self):
            rows = pl.ds(pl.multiple_of(self.row, 16), 16)
            lanes = pl.ds(pl.multiple_of(self.lane, 128), 128)
            here = out.at[self.t0 : self.t0 + self.n, rows, lanes]
            for k in (1, 3, 2):
                self.send(here, here, "gather second", self.second(k))

        def gather_first(self):
            here = self.out_rows(self.f)
            for k in (1, 3) if self.group in RELAYED else (1, 3, 2):
                self.send(here, here, ("gather first", k), self.first(k))
            self.send(here, here, "core", partner)

        def relay(self, k):
            f = (self.f + 4 - k) % 4
            if self.group in RELAYED:
                half = pl.ds(pl.multiple_of(c * 128 + 32 * f + 16 * (k // 2), 16), 16)
                here = out.at[self.t0 : self.t0 + self.n, half]
                self.send(here, here, ("gather first", 2), self.first(k))
            self.gather_core(k)

        def gather_core(self, k):
            here = self.out_rows((self.f + 4 - k) % 4)
            self.send(here, here, "core", partner)

    class Group:
        def __init__(self, index):
            self.i = index
            self.streams = [Stream(index, half) for half in range(2)]

        def send(self, src, dst, name, device):
            send(src, dst, ("sent", self.i), (name, self.i), device)

        def start_first(self):
            for stream in self.streams:
                stream.start_first()

        def start_second(self):
            wait(("first", self.i))
            for stream in self.streams:
                stream.start_second()

        def start_third(self):
            wait(("second", self.i))
            for stream in self.streams:
                stream.sum_second()
            end = self.streams[1].tile0 + self.streams[1].n
            if end < 8:
                z1[self.i, end:8] = jnp.zeros((8 - end, 16, 128), BF)
            for k in (4, 3, 5, 2, 6, 1, 7):
                self.send(z1.at[self.i, (z + k) % 8], r3.at[self.i, k - 1], "third", on_z(k))

        def gather_third(self):
            wait(("third", self.i))
            total = z1[self.i, z].astype(F32)
            for k in range(7):
                total = total + r3[self.i, k].astype(F32)
            a, b = self.streams
            later = (z + 8 - b.tile0) // 8
            rows = pl.ds(pl.multiple_of(a.row + later * (b.row - a.row), 16), 16)
            lanes = pl.ds(pl.multiple_of(a.lane + later * (b.lane - a.lane), 128), 128)
            out[8 * self.i + z, rows, lanes] = total.astype(BF)
            here = out.at[8 * self.i + z, rows, lanes]
            for k in (4, 3, 5, 2, 6, 1, 7):
                self.send(here, here, "gather third", on_z(k))

        def gather_second(self):
            wait(("gather third", self.i))
            for stream in self.streams:
                stream.gather_second()

        def gather_first(self):
            wait(("gather second", self.i))
            for stream in self.streams:
                stream.gather_first()

        def relay(self):
            for k in (1, 3):
                wait((("gather first", k), self.i))
                for stream in self.streams:
                    stream.relay(k)

        def gather_core(self):
            wait((("gather first", 2), self.i))
            for stream in self.streams:
                stream.gather_core(2)

        def finish(self):
            wait(("core", self.i))

    groups = [Group(i) for i in range(len(GROUPS))]

    def grad_rows(s, p):
        a = p + 1 - c
        return gp[a, 32:288] if s == 1 else gs[s // 2, a, 32:288]

    both_planes = [jnp.concatenate([grad_rows(s, 0), grad_rows(s, 1)], axis=0) for s in range(3)]
    for t in range(CONV_TAPS):
        a, b, s = t // 9, (t // 3) % 3, t % 3
        lhs = jnp.concatenate([ht[b, a], ht[b, a + 1]], axis=1)
        sums[t] = dot(lhs, both_planes[s]).astype(BF)
        if t < 24 and t % 4 == 3:
            groups[t // 8].streams[t // 4 % 2].start_first()

    for name in (("grad", 2, False), ("grad", 0, False), ("grad", 1, False), ("grad", 1, True)):
        wait(name)
    away = 2 * c
    clear(gp, (away,), slice(32, 288), other_ok)
    for i, shift in ((0, after), (1, before)):
        gs[i, away, 32:288] = dot(shift, gp[away, 32:288]).astype(BF)
    for plane, valid in ((1, None), (near, None), (away, other_ok)):
        for rows, ok in edges:
            clear(gp, (plane,), rows, ok if valid is None else jnp.logical_and(ok, valid))
            for i, shift in ((0, after), (1, before)):
                gs[i, plane, rows] = dot(shift[0:32, 0:32], gp[plane, rows]).astype(BF)
    back = cotangent
    for a in range(3):
        for b in range(3):
            rows = slice(32 * (2 - b), 32 * (2 - b) + 256)
            for s in range(3):
                piece = gp[2 - a, rows] if s == 1 else gs[s // 2, 2 - a, rows]
                back = back + dot_t(piece, conv_w[9 * a + 3 * b + s])
    hidden_grad = back.astype(BF)
    for t in range(4):
        part[t] = dot(x_t[4 * (1 - c) + t], hidden_grad).astype(BF)
    send(part, part_in, "halo sent", "part", partner)

    unsort = ones_where(row == target(col))

    def write_fine(a):
        flat = [dot_t(hidden_grad, down_w[4 * a + g]).astype(BF) for g in range(4)]
        for block in range(4):
            rows = jnp.concatenate([f[64 * block : 64 * block + 64] for f in flat], axis=0)
            fine_out[a, 4 * block : 4 * block + 4] = dot(unsort, rows).astype(BF).reshape(4, 64, 128)

    groups[0].start_second()
    own = [dot(x_t[4 * c + t], hidden_grad) for t in range(4)]
    wait("part")
    for t in range(4):
        sums[27 + t] = (own[t] + part_in[t].astype(F32)).astype(BF)
    groups[1].start_second()
    groups[3].start_first()
    groups[0].start_third()
    groups[2].start_second()
    groups[1].start_third()
    write_fine(0)
    write_fine(1)
    groups[3].start_second()
    groups[2].start_third()
    groups[0].gather_third()
    groups[1].gather_third()
    groups[3].start_third()
    groups[2].gather_third()
    groups[0].gather_second()
    groups[1].gather_second()
    groups[3].gather_third()
    groups[0].gather_first()
    groups[2].gather_second()
    groups[1].gather_first()
    groups[3].gather_second()
    groups[0].relay()
    groups[2].gather_first()
    groups[1].relay()
    groups[3].gather_first()
    groups[0].gather_core()
    groups[2].relay()
    groups[1].gather_core()
    groups[3].relay()
    groups[2].gather_core()
    groups[3].gather_core()
    for group in groups:
        group.finish()
    wait_all()


def deliver(fine, sums, fine_out, conv_out, down_out, sems):
    moves = [(sums.at[t : t + 9], conv_out.at[t : t + 9]) for t in range(0, CONV_TAPS, 9)]
    moves.append((fine, fine_out))
    for core in range(2):
        taps = sums.at[CONV_TAPS : CONV_TAPS + 4, 128 * core : 128 * core + 128]
        moves.append((taps, down_out.at[4 * core : 4 * core + 4]))
    copies = []
    for i, (src, dst) in enumerate(moves):
        copy = pltpu.make_async_copy(src, dst, sems.at[i])
        copy.start()
        copies.append(copy)
    for copy in copies:
        copy.wait()


def on_device(fine_field, down_weight, conv_weight, coarse_cotangent):
    vmem = pl.BlockSpec(memory_space=pltpu.VMEM)
    groups, streams = len(GROUPS), 2 * len(GROUPS)
    operands = (fine_field, down_weight, conv_weight, coarse_cotangent)
    operands = [pltpu.with_memory_space_constraint(x, pltpu.HBM) for x in operands]
    results = pl.pallas_call(
        kernel,
        out_shape=(
            jax.ShapeDtypeStruct(fine_field.shape, BF),
            jax.ShapeDtypeStruct((32, 256, 256), BF),
        ),
        in_specs=[pl.BlockSpec(memory_space=pltpu.HBM)] * 4,
        out_specs=(vmem, vmem),
        scratch_shapes=[
            pltpu.VMEM(fine_field.shape, BF),
            pltpu.VMEM(down_weight.shape, BF),
            pltpu.VMEM(conv_weight.shape, BF),
            pltpu.VMEM(coarse_cotangent.shape, BF),
            pltpu.VMEM((256, 1024), BF),
            pltpu.VMEM((8, 128, 256), BF),
            pltpu.VMEM((4, 2, 320, 128), BF),
            pltpu.VMEM((2, 3, 320, 256), BF),
            pltpu.VMEM((3, 4, 128, 256), BF),
            pltpu.VMEM((3, 320, 256), BF),
            pltpu.VMEM((2, 3, 320, 256), BF),
            pltpu.VMEM((31, 128, 256), BF),
            pltpu.VMEM((4, 128, 256), BF),
            pltpu.VMEM((4, 128, 256), BF),
            pltpu.VMEM((streams, 3, MOST, 32, 256), BF),
            pltpu.VMEM((streams, MOST, 32, 256), BF),
            pltpu.VMEM((streams, 3, MOST, 16, 128), BF),
            pltpu.VMEM((groups, 8, 16, 128), BF),
            pltpu.VMEM((groups, 7, 16, 128), BF),
            pltpu.VMEM((864, 16, 128), BF),
            pltpu.SemaphoreType.DMA((SEMAPHORES,)),
        ],
        compiler_params=pltpu.CompilerParams(
            collective_id=0, has_side_effects=True, vmem_limit_bytes=36 * 1024 * 1024
        ),
        name="section_backward",
    )(*operands)
    hbm = pl.BlockSpec(memory_space=pltpu.HBM)
    return pl.pallas_call(
        deliver,
        out_shape=tuple(jax.ShapeDtypeStruct(x.shape, BF) for x in (fine_field, conv_weight, down_weight)),
        in_specs=[vmem] * 2,
        out_specs=(hbm, hbm, hbm),
        scratch_shapes=[pltpu.SemaphoreType.DMA((6,))],
        compiler_params=pltpu.CompilerParams(vmem_limit_bytes=1024 * 1024),
        name="deliver",
    )(*[pltpu.with_memory_space_constraint(r, pltpu.VMEM) for r in results])


def solution(mesh):
    in_specs = (P("gx", "gy", None, None), P(), P(), P("gx", "gy", None, None))
    out_specs = (P("gx", "gy", None, None), P(), P())
    return jax.shard_map(
        on_device, mesh=mesh, in_specs=in_specs, out_specs=out_specs, check_vma=False
    )
```
